128 devices in a mesh: exp: 8 (over x, core), row: 4 (over z), col: 4 (over y).
Axes of the slice: x: 4, y: 4, z: 4, core: 2. Of those that a mesh axis runs over, the one named last changes fastest.
Arguments:
- grad_out: bfloat16 [4096, 6144], P(('exp', 'row'), 'col'), may hold values from -6 to 6
- routes: int32 [4096, 2], P(('exp', 'row')), may hold values from 0 to 7, all different within a row; in each aligned block of 128 rows (0 to 127, 128 to 255, ...) at most 40 rows name the same one
- combine: float32 [4096, 2], P(('exp', 'row')), may hold values from 0.2 to 1
- w_gate: bfloat16 [8, 6144, 8192], P('exp', None, ('row', 'col')), may hold values from -0.078125 to 0.078125
- w_up: bfloat16 [8, 6144, 8192], P('exp', None, ('row', 'col')), may hold values from -0.078125 to 0.078125
- w_down: bfloat16 [8, 8192, 6144], P('exp', ('row', 'col')), may hold values from -0.0625 to 0.0625
- stash_gate: bfloat16 [4, 8, 8, 40, 8192], P(None, None, 'exp', None, ('row', 'col')), may hold values from -4 to 4
- stash_up: bfloat16 [4, 8, 8, 40, 8192], P(None, None, 'exp', None, ('row', 'col')), may hold values from -4 to 4
- stash_scale: float32 [2, 4, 8, 8, 40], P(None, None, None, 'exp'), may hold values from 0.4 to 2.5
Outputs:
- input_grad: bfloat16 [4096, 6144], P(('exp', 'row'), 'col')
The draws below stay inside these ranges and needn't reach their ends.
Inputs may be any that keep to these rules, and one draw needn't show every extreme that they name: `routes`: each row names two different experts. Within each aligned block of 128 rows (the rows of one device) no expert is named by more than 40 rows, and in every draw some expert is named by exactly 40 rows of some block.
All inputs are finite; a program needn't handle non-finite values.
Results may differ from the reference program's by a relative error of at most 0.02.
Values may be sent and summed in bfloat16 or wider, within the bound.
No kernel may reach another device: no remote copies, remote signals or barrier semaphores. Data moves between devices by JAX's collectives and lax.ppermute only.
A program may use at most 192 MiB of HBM per device.

```python
import math
import jax
import jax.numpy as jnp
import numpy as np
from jax import lax

D = 6144
FF = 8192
EXPERTS = 8
TOK_DEV = 128
CAP = 40
ROW_DEVS = 4
COL_DEVS = 4
EXP_DEVS = 8
TOKENS = 4096


def level_of(own_key, extent, cuts, low, high):
    level, own = 1.0, jax.random.fold_in(own_key, 6)
    for dim, blocks in cuts:
        draws = jnp.exp(jax.random.uniform(jax.random.fold_in(own, dim), (blocks,), jnp.float32, low / len(cuts), high / len(cuts)))
        level = level * jnp.repeat(draws, extent[dim] // blocks).reshape([-1 if axis == dim else 1 for axis in range(len(extent))])
    return level


def deal_out(key, own, number, rows, count, top, reach, skew):
    order = jax.random.permutation(key, count)
    packed, usual = load_shares(count, rows * top, reach, skew, True), load_shares(count, rows * top, reach, skew, False)
    places = jnp.arange(count)

    def named(lengths, turn):
        used = int((lengths > 0).sum())
        fixed = max(1, used // 4)
        shifted = fixed + (places - fixed + turn * (used - fixed)) % max(1, count - fixed)
        return jnp.zeros((count,), jnp.int32).at[order[jnp.where(places < fixed, places, shifted)]].set(jnp.asarray(lengths, jnp.int32))

    lengths = jnp.where(number % 4 == 0, named(packed, number // 4), named(usual, number - number // 4 - 1))
    mixed = jax.random.permutation(jax.random.fold_in(own, 3), count)
    source_of, receiver = mixed[0:count // 2 * 2:2], mixed[1:count // 2 * 2:2]
    room = jnp.minimum(lengths[source_of] - 1, reach - lengths[receiver]) // 2
    room = jnp.where((source_of == order[0]) | (receiver == order[0]) | (lengths[receiver] == 0), 0, jnp.maximum(room, 0))
    shifted = jax.random.randint(jax.random.fold_in(own, 4), (count // 2,), 0, 1 << 20) % (room + 1)
    lengths = lengths.at[source_of].add(-shifted).at[receiver].add(shifted)
    members = jnp.searchsorted(jnp.cumsum(lengths), jnp.arange(rows * top), side="right").astype(jnp.int32)
    table = members.reshape(top, rows).T
    table = table[jax.random.permutation(jax.random.fold_in(own, 1), rows)]
    turn = jax.random.randint(jax.random.fold_in(own, 2), (rows, 1), 0, top)
    return jnp.take_along_axis(table, (jnp.arange(top)[None, :] + turn) % top, axis=1)


def load_shares(count, total, most, slope, full):
    loads = [(1 << 20) // math.isqrt(grade ** slope) + 1 for grade in range(1, count + 1)]
    largest = most if full else min(most, max(-(-total // count), total * loads[0] // sum(loads)))
    least = 1 if total - largest >= count - 1 else 0
    holding, spare = [largest] + [least] * (count - 1), total - largest - least * (count - 1)
    while spare > 0:
        free = [i for i in range(1, count) if holding[i] < largest] or [i for i in range(1, count) if holding[i] < most]
        whole, remaining = sum([loads[i] for i in free]), spare
        for i in free:
            extra = min(most - holding[i], max(1, remaining * loads[i] // whole), spare)
            holding[i] = holding[i] + extra
            spare = spare - extra
    return np.array(holding)


def noise(rng, extent, spread, limit, pieces=(), kind=jnp.bfloat16):
    values = spread * jax.random.normal(rng, extent, jnp.float32)
    if pieces:
        values = values * level_of(rng, extent, pieces, -0.22, 0.18)
    return jnp.clip(values, -limit, limit).astype(kind)


def setup_inputs(seed: int = 0) -> dict:
    keys = jax.random.split(jax.random.key(seed), 10)
    grad_out = noise(keys[0], (TOKENS, D), 1.0, 6.0, ((0, 32), (1, 4)))
    routes_keys = jax.random.split(jax.random.fold_in(keys[1], 1), TOKENS // TOK_DEV)
    routes_turns = jax.random.permutation(jax.random.fold_in(keys[1], 3), TOKENS // TOK_DEV)
    routes = jax.vmap(lambda own, number: deal_out(jax.random.fold_in(keys[1], 2), own, number, TOK_DEV, EXPERTS, 2, CAP, 2))(routes_keys, routes_turns).reshape((TOKENS, 2))
    combine = jnp.clip(0.2 + 0.8 * jax.random.uniform(keys[2], (TOKENS, 2), jnp.float32) ** level_of(keys[2], (TOKENS, 2), ((0, 32),), -0.2, 0.2), 0.2, 1.0)
    w_gate = noise(keys[3], (EXPERTS, D, FF), D ** -0.5, 0.078125, ((0, 8), (2, 16)))
    w_up = noise(keys[4], (EXPERTS, D, FF), D ** -0.5, 0.078125, ((0, 8), (2, 16)))
    w_down = noise(keys[5], (EXPERTS, FF, D), FF ** -0.5, 0.0625, ((0, 8), (1, 16)))
    stash_gate = noise(keys[6], (ROW_DEVS, EXP_DEVS, EXPERTS, CAP, FF), 1.0, 4.0, ((2, 8), (4, 16)))
    stash_up = noise(keys[7], (ROW_DEVS, EXP_DEVS, EXPERTS, CAP, FF), 1.0, 4.0, ((2, 8), (4, 16)))
    stash_scale = jnp.clip(jnp.exp(math.log(2.5) - 1.8325814 * jax.random.uniform(keys[8], (2, ROW_DEVS, EXP_DEVS, EXPERTS, CAP), jnp.float32) ** level_of(keys[8], (2, ROW_DEVS, EXP_DEVS, EXPERTS, CAP), ((3, 8),), -0.2, 0.2)), 0.4, 2.5)
    return {"grad_out": grad_out, "routes": routes, "combine": combine, "w_gate": w_gate, "w_up": w_up, "w_down": w_down, "stash_gate": stash_gate, "stash_up": stash_up, "stash_scale": stash_scale}


def slot_positions(routes):
    blocks = routes.reshape(TOKENS // TOK_DEV, TOK_DEV * 2)
    onehot = (blocks[:, :, None] == jnp.arange(EXPERTS, dtype=jnp.int32)[None, None, :]).astype(jnp.int32)
    before = jnp.cumsum(onehot, axis=1) - onehot
    return jnp.sum(before * onehot, axis=2).reshape(TOKENS, 2).astype(jnp.int32)


def expert_backward(operands):
    rows, gate_weight, up_weight, down_weight, stored_gate, stored_up, gate_scale, up_scale = operands
    flat_rows = rows.reshape(-1, D)
    hidden_grad = jnp.dot(flat_rows, down_weight.T, preferred_element_type=jnp.float32)
    gate_pre = stored_gate.reshape(-1, FF).astype(jnp.float32) * gate_scale.reshape(-1, 1)
    up_pre = stored_up.reshape(-1, FF).astype(jnp.float32) * up_scale.reshape(-1, 1)
    sigmoid_gate = jax.nn.sigmoid(gate_pre)
    up_grad = (hidden_grad * gate_pre * sigmoid_gate).astype(jnp.bfloat16)
    gate_grad = (hidden_grad * up_pre * sigmoid_gate * (1.0 + gate_pre * (1.0 - sigmoid_gate))).astype(jnp.bfloat16)
    groups = ROW_DEVS * COL_DEVS
    group_width = FF // groups
    total = jnp.zeros((flat_rows.shape[0], D), jnp.float32)
    for group in range(groups):
        first = group * group_width
        last = first + group_width
        group_term = jnp.dot(gate_grad[:, first:last], gate_weight[:, first:last].T, preferred_element_type=jnp.float32)
        group_term = group_term + jnp.dot(up_grad[:, first:last], up_weight[:, first:last].T, preferred_element_type=jnp.float32)
        rounded = lax.optimization_barrier(group_term.astype(jnp.bfloat16))
        total = total + rounded.astype(jnp.float32)
    return total.astype(jnp.bfloat16).reshape(rows.shape)


def reference(grad_out, routes, combine, w_gate, w_up, w_down, stash_gate, stash_up, stash_scale):
    slot_index = slot_positions(routes)
    token_ids = jnp.arange(TOKENS, dtype=jnp.int32)
    block_ids = token_ids // TOK_DEV
    row_ids = jnp.broadcast_to((block_ids % ROW_DEVS)[:, None], (TOKENS, 2)).astype(jnp.int32)
    source_ids = jnp.broadcast_to((block_ids // ROW_DEVS)[:, None], (TOKENS, 2)).astype(jnp.int32)
    scaled = (combine[:, :, None] * grad_out[:, None, :].astype(jnp.float32)).astype(jnp.bfloat16)
    expert_rows = jnp.zeros((EXPERTS, ROW_DEVS, EXP_DEVS, CAP, D), jnp.bfloat16)
    expert_rows = expert_rows.at[routes, row_ids, source_ids, slot_index].set(scaled)
    slot_grad = lax.map(expert_backward, (
        expert_rows, w_gate, w_up, w_down,
        jnp.moveaxis(stash_gate, 2, 0), jnp.moveaxis(stash_up, 2, 0),
        jnp.moveaxis(stash_scale[0], 2, 0), jnp.moveaxis(stash_scale[1], 2, 0)))
    picked = slot_grad[routes, row_ids, source_ids, slot_index].astype(jnp.float32)
    return (picked[:, 0] + picked[:, 1]).astype(jnp.bfloat16)
```

```python
import functools

import jax
import jax.numpy as jnp
from jax import lax
from jax.experimental import pallas as pl
from jax.experimental.pallas import tpu as pltpu
from jax.sharding import PartitionSpec as P

ALL = ("exp", "row", "col")
BF = jnp.bfloat16
F32 = jnp.float32
RING = 4
VMEM = 48 * 1024 * 1024


def all_devices():
    for x in range(4):
        for k in range(2):
            for z in range(4):
                for y in range(4):
                    yield x, k, z, y


def device_id(x, k, z, y):
    return (((x % 4) * 2 + k) * 4 + z % 4) * 4 + y % 4


def receive_from(value, stage, offset):
    pairs = []
    for x, k, z, y in all_devices():
        if k == stage:
            source = device_id(x, k, z, y + offset)
        else:
            source = device_id(x, k, z + offset, y)
        pairs.append((source, device_id(x, k, z, y)))
    return lax.ppermute(value, ALL, pairs)


def receive_along_x(value, offset):
    pairs = [(device_id(x + offset, k, z, y), device_id(x, k, z, y)) for x, k, z, y in all_devices()]
    return lax.ppermute(value, ALL, pairs)


def swap_cores(value):
    pairs = [(device_id(x, 1 - k, z, y), device_id(x, k, z, y)) for x, k, z, y in all_devices()]
    return lax.ppermute(value, ALL, pairs)


def dot_nt(a, b):
    return lax.dot_general(a, b, (((1,), (1,)), ((), ())), preferred_element_type=F32)


def after(value, *others):
    return lax.optimization_barrier((value, *others))[0]


SIDES = (0, 1, 3)
FAR = 2
ANY = pl.BlockSpec(memory_space=pl.ANY)
IN_VMEM = pl.BlockSpec(memory_space=pltpu.VMEM)
IN_SMEM = pl.BlockSpec(memory_space=pltpu.SMEM)


class Copies:
    def __init__(self, sems):
        self.sems, self.used = sems, 0

    def start(self, source, target):
        copy = pltpu.make_async_copy(source, target, self.sems.at[self.used])
        self.used += 1
        copy.start()
        return copy


def block_at(info, offset, narrow):
    return pl.ds(pl.multiple_of(lax.rem(info[1] + offset, RING) * narrow, 128), narrow)


def by_core(info, run):
    for core in range(2):

        @pl.when(info[0] == core)
        def _():
            run(core)


def hidden_kernel(info, *refs):
    pieces, (down, acc, xs, ws, sems) = refs[:6], refs[6:]
    _, rows, narrow = pieces[0].shape

    def run(core):
        copies = Copies(sems)
        steps = []
        for step in range(4 if core == 0 else 3):
            column = step if core == 0 else SIDES[step]
            waits = [copies.start(down.at[:, block_at(info, column, narrow)], ws.at[step])]
            parts = [(s, step) for s in range(3)] if core == 0 else [(step, i1) for i1 in SIDES + (FAR,)]
            first = step * len(parts)
            for n, (s, i1) in enumerate(parts):
                waits.append(
                    copies.start(pieces[2 * s + i1 // 2].at[i1 % 2], xs.at[pl.ds((first + n) * rows, rows)])
                )
            steps.append((step, first * rows, len(parts) * rows, waits))
        for step, first, size, waits in steps:
            for copy in waits:
                copy.wait()
            value = dot_nt(xs[first : first + size, :], ws[step])
            if step == 0:
                acc[:size, :] = value
            else:
                acc[:size, :] += value
        if core == 0:
            acc[3 * rows :, :] = jnp.zeros((rows, acc.shape[1]), F32)

    by_core(info, run)


def hidden_part(info, pieces, w_down, name):
    _, rows, narrow = pieces[0].shape
    hidden = w_down.shape[0]
    return pl.pallas_call(
        hidden_kernel,
        in_specs=[IN_SMEM] + [ANY] * 7,
        out_specs=IN_VMEM,
        out_shape=jax.ShapeDtypeStruct((4 * rows, hidden), F32),
        scratch_shapes=[
            pltpu.VMEM((12 * rows, narrow), BF),
            pltpu.VMEM((4, hidden, narrow), BF),
            pltpu.SemaphoreType.DMA((16,)),
        ],
        compiler_params=pltpu.CompilerParams(vmem_limit_bytes=VMEM),
        cost_estimate=pl.CostEstimate(
            flops=24 * rows * narrow * hidden,
            bytes_accessed=24 * rows * narrow + 2 * w_down.size + 16 * rows * hidden,
            transcendentals=0,
        ),
        name=name,
    )(info, *pieces, w_down)


def product(gg, ug, first, size, gate, up, out, place):
    for n in range(0, out.shape[1], 512):
        value = dot_nt(gg[first : first + size, :], gate[n : n + 512, :])
        value = value + dot_nt(ug[first : first + size, :], up[n : n + 512, :])
        out[place : place + size, n : n + 512] = value.astype(BF)


def far_kernel(info, acc, far_a, far_b, down, fgate, fup, wgate, wup, out_a, out_b, gg, ug,
               xs, ws, sums, factors, gs, us, outs, sems):
    _, rows, narrow = far_a.shape
    far, to = (far_a, far_b), (out_a, out_b)

    def run(core):
        copies = Copies(sems)
        columns = range(4) if core == 0 else (FAR,)
        load_sum = copies.start(acc, sums)
        steps = []
        order = range(4) if core == 0 else SIDES + (FAR,)
        loads = []
        for n, i1 in enumerate(order):
            if n < len(columns):
                loads.append(copies.start(down.at[:, block_at(info, columns[n], narrow)], ws.at[n]))
            loads.append(copies.start(far[i1 // 2].at[i1 % 2], xs.at[pl.ds(n * rows, rows)]))
        load_factors = [copies.start(fgate, factors.at[0]), copies.start(fup, factors.at[1])]
        weights = []
        for n, column in enumerate(columns):
            block = block_at(info, column, narrow)
            weights.append([copies.start(wgate.at[block], gs.at[n]), copies.start(wup.at[block], us.at[n])])
        load_sum.wait()
        for copy in loads:
            copy.wait()
        if core == 0:
            value = sums[3 * rows :, :]
            for n in range(4):
                value = value + dot_nt(xs[n * rows : (n + 1) * rows, :], ws[n])
            sums[3 * rows :, :] = value
        else:
            sums[...] += dot_nt(xs[...], ws[0])
        for copy in load_factors:
            copy.wait()
        gg[...] = (sums[...] * factors[0]).astype(BF)
        ug[...] = (sums[...] * factors[1]).astype(BF)
        stores = []
        for n in range(len(columns)):
            for copy in weights[n]:
                copy.wait()
            if core == 0:
                product(gg, ug, 3 * rows, rows, gs.at[n], us.at[n], outs, n * rows)
                parts = [(n, n)]
            else:
                product(gg, ug, 0, 4 * rows, gs.at[n], us.at[n], outs, 0)
                parts = list(enumerate(order))
            for place, i1 in parts:
                stores.append(copies.start(outs.at[pl.ds(place * rows, rows)], to[i1 // 2].at[i1 % 2]))
        for copy in stores:
            copy.wait()

    by_core(info, run)


def far_part(info, acc, far_a, far_b, w_down, factor_gate, factor_up, w_gate, w_up, name):
    _, rows, narrow = far_a.shape
    hidden = w_down.shape[0]
    return pl.pallas_call(
        far_kernel,
        in_specs=[IN_SMEM] + [ANY] * 8,
        out_specs=[ANY, ANY, IN_VMEM, IN_VMEM],
        out_shape=[
            jax.ShapeDtypeStruct((2, rows, narrow), BF),
            jax.ShapeDtypeStruct((2, rows, narrow), BF),
            jax.ShapeDtypeStruct((4 * rows, hidden), BF),
            jax.ShapeDtypeStruct((4 * rows, hidden), BF),
        ],
        scratch_shapes=[
            pltpu.VMEM((4 * rows, narrow), BF),
            pltpu.VMEM((4, hidden, narrow), BF),
            pltpu.VMEM((4 * rows, hidden), F32),
            pltpu.VMEM((2, 4 * rows, hidden), F32),
            pltpu.VMEM((4, narrow, hidden), BF),
            pltpu.VMEM((4, narrow, hidden), BF),
            pltpu.VMEM((4 * rows, narrow), BF),
            pltpu.SemaphoreType.DMA((24,)),
        ],
        compiler_params=pltpu.CompilerParams(vmem_limit_bytes=VMEM),
        cost_estimate=pl.CostEstimate(
            flops=24 * rows * narrow * hidden,
            bytes_accessed=16 * rows * narrow + 6 * w_down.size + 64 * rows * hidden,
            transcendentals=0,
        ),
        name=name,
    )(info, acc, far_a, far_b, w_down, factor_gate, factor_up, w_gate, w_up)


def sides_kernel(info, gg, ug, wgate, wup, *refs):
    pieces, (gs, us, outs, sems) = refs[:6], refs[6:]
    _, rows, narrow = pieces[0].shape

    def run(core):
        copies = Copies(sems)
        columns = range(4) if core == 0 else SIDES
        weights, stores = [], []
        for n, column in enumerate(columns):
            block = block_at(info, column, narrow)
            weights.append([copies.start(wgate.at[block], gs.at[n]), copies.start(wup.at[block], us.at[n])])
        for n in range(len(columns)):
            for copy in weights[n]:
                copy.wait()
            parts = [(s, n) for s in range(3)] if core == 0 else [(n, i1) for i1 in SIDES + (FAR,)]
            first, size = n * len(parts) * rows, len(parts) * rows
            product(gg, ug, 0, size, gs.at[n], us.at[n], outs, first)
            for m, (s, i1) in enumerate(parts):
                stores.append(
                    copies.start(outs.at[pl.ds(first + m * rows, rows)], pieces[2 * s + i1 // 2].at[i1 % 2])
                )
        for copy in stores:
            copy.wait()

    by_core(info, run)


def sides_part(info, gate_grad, up_grad, w_gate, w_up, name):
    rows, hidden = gate_grad.shape[0] // 4, gate_grad.shape[1]
    narrow = w_gate.shape[0] // RING
    return pl.pallas_call(
        sides_kernel,
        in_specs=[IN_SMEM, IN_VMEM, IN_VMEM, ANY, ANY],
        out_specs=[ANY] * 6,
        out_shape=[jax.ShapeDtypeStruct((2, rows, narrow), BF)] * 6,
        scratch_shapes=[
            pltpu.VMEM((4, narrow, hidden), BF),
            pltpu.VMEM((4, narrow, hidden), BF),
            pltpu.VMEM((12 * rows, narrow), BF),
            pltpu.SemaphoreType.DMA((20,)),
        ],
        compiler_params=pltpu.CompilerParams(vmem_limit_bytes=VMEM),
        cost_estimate=pl.CostEstimate(
            flops=48 * rows * narrow * hidden,
            bytes_accessed=24 * rows * narrow + 4 * w_gate.size,
            transcendentals=0,
        ),
        name=name,
    )(info, gate_grad, up_grad, w_gate, w_up)


def relative_order(array, x, core, row):
    array = array.reshape((4, 4, 2) + array.shape[2:])
    array = lax.dynamic_slice_in_dim(jnp.concatenate([array, array], axis=0), row, 4, axis=0)
    array = lax.dynamic_slice_in_dim(jnp.concatenate([array, array], axis=1), x, 4, axis=1)
    array = jnp.stack([array[n] for n in SIDES + (FAR,)])
    return jnp.where(core == 0, array, array[:, :, ::-1])


def gather_small(rows):
    return [
        rows,
        receive_from(rows, 0, 1),
        receive_from(rows, 0, 2),
        receive_from(rows, 0, 3),
    ]


def body(grad_out, routes, combine, w_gate, w_up, w_down, stash_gate, stash_up, stash_scale):
    exp = lax.axis_index("exp")
    row = lax.axis_index("row")
    col = lax.axis_index("col")
    x, core = exp // 2, exp % 2
    w_gate, w_up, w_down = w_gate[0], w_up[0], w_down[0]
    capacity = stash_gate.shape[3]
    tokens, narrow = grad_out.shape
    hidden = w_gate.shape[1]

    flat = routes.reshape(-1)
    onehot = (flat[:, None] == jnp.arange(8, dtype=jnp.int32)[None, :]).astype(jnp.int32)
    before = jnp.cumsum(onehot, axis=0) - onehot
    slot_index = jnp.sum(before * onehot, axis=1)
    place = ((flat % 2) ^ core) * 4 + (x - flat // 2) % 4
    target = place * capacity + slot_index
    matches = jnp.arange(8 * capacity, dtype=jnp.int32)[:, None] == target[None, :]
    matches = matches.reshape(8 * capacity, tokens, 2)
    picker = jnp.any(matches, axis=2).astype(BF)
    weight = jnp.sum(jnp.where(matches, combine[None, :, :], 0.0), axis=(1, 2))
    copied = jnp.dot(picker, grad_out, preferred_element_type=F32)
    slots = (copied * weight[:, None]).astype(BF).reshape(2, 4, capacity, narrow)

    other = swap_cores(slots[1])
    held = jnp.stack([slots[0], other], axis=1)
    near = held[0].reshape(2 * capacity, narrow)
    arrived = [receive_along_x(held[j], j) for j in (1, 3, 2)]

    stash = [relative_order(array[:, :, 0], x, core, row) for array in (stash_gate, stash_up)]
    scale = [relative_order(stash_scale[n, :, :, 0], x, core, row) for n in range(2)]

    def factors_of(part):
        gate_pre = stash[0][:, part].astype(F32) * scale[0][:, part, ..., None]
        up_pre = stash[1][:, part].astype(F32) * scale[1][:, part, ..., None]
        sigmoid_gate = jax.nn.sigmoid(gate_pre)
        factor_up = gate_pre * sigmoid_gate
        factor_gate = up_pre * sigmoid_gate * (1.0 + gate_pre * (1.0 - sigmoid_gate))
        return factor_gate.reshape(-1, hidden), factor_up.reshape(-1, hidden)

    near_factors = factors_of(slice(0, 1))
    rest_factors = factors_of(slice(1, 4))
    info = jnp.stack([core, col]).astype(jnp.int32)

    def gather_near(small, wait_for):
        own_a, own_b = jnp.stack(small[:2]), jnp.stack(small[2:])
        if wait_for:
            own_a, own_b, *_ = lax.optimization_barrier((own_a, own_b, *wait_for))
        plus_a, minus_b = receive_from(own_a, 1, 1), receive_from(own_b, 1, 3)
        plus_b, minus_a = receive_from(own_b, 1, 1), receive_from(own_a, 1, 3)
        return own_a, own_b, plus_a, plus_b, minus_a, minus_b

    def gather_far(plus_a, minus_b):
        return receive_from(plus_a, 1, 1), receive_from(minus_b, 1, 3)

    near_small = gather_small(near)
    near_pieces = gather_near(near_small, [])
    near_far = gather_far(near_pieces[2], near_pieces[5])
    rest = jnp.stack([arrived[0], arrived[2], arrived[1]]).reshape(6 * capacity, narrow)
    rest = after(rest, *near_small)
    rest_pieces = gather_near(gather_small(rest), near_pieces[2:])

    near_acc = hidden_part(info, near_pieces, w_down, "hidden_near")
    near_out = far_part(info, near_acc, *near_far, w_down, *near_factors, w_gate, w_up, "far_near")
    near_far_out = near_out[:2]
    rest_far = gather_far(*lax.optimization_barrier((rest_pieces[2], rest_pieces[5], *near_out))[:2])
    near_terms = sides_part(info, near_out[2], near_out[3], w_gate, w_up, "sides_near")
    rest_acc = hidden_part(
        info, lax.optimization_barrier((*rest_pieces, *near_terms))[:6], w_down, "hidden_rest"
    )
    rest_out = far_part(info, rest_acc, *rest_far, w_down, *rest_factors, w_gate, w_up, "far_rest")

    def scatter_far(out_a, out_b):
        return receive_from(out_a, 1, 3), receive_from(out_b, 1, 1)

    def add(a, b):
        return (a.astype(F32) + b.astype(F32)).astype(BF)

    def scatter_near(terms, got):
        own_a, own_b, plus_a, plus_b, minus_a, minus_b = terms
        back_b, ahead_a = receive_from(plus_b, 1, 3), receive_from(minus_a, 1, 1)
        back_a, ahead_b = receive_from(add(plus_a, got[0]), 1, 3), receive_from(add(minus_b, got[1]), 1, 1)
        parts = ((own_a, back_a, ahead_a), (own_b, back_b, ahead_b))
        return [
            (own[n].astype(F32) + back[n].astype(F32) + ahead[n].astype(F32)).astype(BF)
            for own, back, ahead in parts
            for n in range(2)
        ]

    def scatter_small(total):
        got = [receive_from(total[1], 0, 3), receive_from(total[2], 0, 2), receive_from(total[3], 0, 1)]
        summed = total[0].astype(F32)
        for part in got:
            summed = summed + part.astype(F32)
        return summed.astype(BF)

    rest_got = scatter_far(rest_out[0], rest_out[1])
    rest_terms = sides_part(info, rest_out[2], rest_out[3], w_gate, w_up, "sides_rest")
    rest_got = lax.optimization_barrier((*rest_got, *rest_terms))[:2]
    near_got = scatter_far(*lax.optimization_barrier((*near_far_out, *rest_got))[:2])
    rest_sum = scatter_small(scatter_near(rest_terms, rest_got)).reshape(3, 2, capacity, narrow)
    near_sum = scatter_small(scatter_near(near_terms, near_got)).reshape(1, 2, capacity, narrow)

    back = jnp.stack([receive_along_x(rest_sum[j - 1], -j) for j in (1, 2, 3)])
    returned = jnp.concatenate(
        [near_sum[:, 0], back[:, 0], swap_cores(near_sum[:, 1]), swap_cores(back[:, 1])], axis=0
    ).reshape(8 * capacity, narrow)
    result = lax.dot_general(picker, returned, (((0,), (0,)), ((), ())), preferred_element_type=F32)
    return result.astype(BF)


def solution(mesh):
    placed = (
        P(("exp", "row"), "col"),
        P(("exp", "row"), None),
        P(("exp", "row"), None),
        P("exp", None, ("row", "col")),
        P("exp", None, ("row", "col")),
        P("exp", ("row", "col"), None),
        P(None, None, "exp", None, ("row", "col")),
        P(None, None, "exp", None, ("row", "col")),
        P(None, None, None, "exp", None),
    )
    return jax.shard_map(
        body, mesh=mesh, in_specs=placed, out_specs=P(("exp", "row"), "col"), check_vma=False
    )
```

```python
import functools

import jax
import jax.numpy as jnp
from jax import lax
from jax.experimental import pallas as pl
from jax.experimental.pallas import tpu as pltpu
from jax.sharding import PartitionSpec as P

ALL = ("exp", "row", "col")
BF = jnp.bfloat16
F32 = jnp.float32
RING = 4
VMEM = 60 * 1024 * 1024


def all_devices():
    for x in range(4):
        for k in range(2):
            for z in range(4):
                for y in range(4):
                    yield x, k, z, y


def device_id(x, k, z, y):
    return (((x % 4) * 2 + k) * 4 + z % 4) * 4 + y % 4


def receive_from(value, stage, offset):
    pairs = []
    for x, k, z, y in all_devices():
        if k == stage:
            source = device_id(x, k, z, y + offset)
        else:
            source = device_id(x, k, z + offset, y)
        pairs.append((source, device_id(x, k, z, y)))
    return lax.ppermute(value, ALL, pairs)


def receive_along_x(value, offset):
    pairs = [(device_id(x + offset, k, z, y), device_id(x, k, z, y)) for x, k, z, y in all_devices()]
    return lax.ppermute(value, ALL, pairs)


def swap_cores(value):
    pairs = [(device_id(x, 1 - k, z, y), device_id(x, k, z, y)) for x, k, z, y in all_devices()]
    return lax.ppermute(value, ALL, pairs)


def dot_nt(a, b):
    return lax.dot_general(a, b, (((1,), (1,)), ((), ())), preferred_element_type=F32)


def after(value, *others):
    return lax.optimization_barrier((value, *others))[0]


SIDES = (0, 1, 3)
FAR = 2
ANY = pl.BlockSpec(memory_space=pl.ANY)
IN_VMEM = pl.BlockSpec(memory_space=pltpu.VMEM)
IN_SMEM = pl.BlockSpec(memory_space=pltpu.SMEM)


class Copies:
    def __init__(self, sems):
        self.sems, self.used = sems, 0

    def start(self, source, target):
        copy = pltpu.make_async_copy(source, target, self.sems.at[self.used])
        self.used += 1
        copy.start()
        return copy


def block_at(info, offset, narrow):
    return pl.ds(pl.multiple_of(lax.rem(info[1] + offset, RING) * narrow, 128), narrow)


def by_core(info, run):
    for core in range(2):

        @pl.when(info[0] == core)
        def _():
            run(core)


def hidden_kernel(info, *refs):
    pieces, (down, acc, xs, ws, sems) = refs[:6], refs[6:]
    _, rows, narrow = pieces[0].shape

    def run(core):
        copies = Copies(sems)
        steps = []
        for step in range(4 if core == 0 else 3):
            column = step if core == 0 else SIDES[step]
            waits = [copies.start(down.at[:, block_at(info, column, narrow)], ws.at[step])]
            parts = [(s, step) for s in range(3)] if core == 0 else [(step, i1) for i1 in SIDES + (FAR,)]
            first = step * len(parts)
            for n, (s, i1) in enumerate(parts):
                waits.append(
                    copies.start(pieces[2 * s + i1 // 2].at[i1 % 2], xs.at[pl.ds((first + n) * rows, rows)])
                )
            steps.append((step, first * rows, len(parts) * rows, waits))
        for step, first, size, waits in steps:
            for copy in waits:
                copy.wait()
            value = dot_nt(xs[first : first + size, :], ws[step])
            if step == 0:
                acc[:size, :] = value
            else:
                acc[:size, :] += value
        if core == 0:
            acc[3 * rows :, :] = jnp.zeros((rows, acc.shape[1]), F32)

    by_core(info, run)


def hidden_part(info, pieces, w_down, name):
    _, rows, narrow = pieces[0].shape
    hidden = w_down.shape[0]
    return pl.pallas_call(
        hidden_kernel,
        in_specs=[IN_SMEM] + [ANY] * 7,
        out_specs=IN_VMEM,
        out_shape=jax.ShapeDtypeStruct((4 * rows, hidden), F32),
        scratch_shapes=[
            pltpu.VMEM((12 * rows, narrow), BF),
            pltpu.VMEM((4, hidden, narrow), BF),
            pltpu.SemaphoreType.DMA((16,)),
        ],
        compiler_params=pltpu.CompilerParams(vmem_limit_bytes=VMEM),
        cost_estimate=pl.CostEstimate(
            flops=24 * rows * narrow * hidden,
            bytes_accessed=24 * rows * narrow + 2 * w_down.size + 16 * rows * hidden,
            transcendentals=0,
        ),
        name=name,
    )(info, *pieces, w_down)


def product(grads, first, size, weights, out, place):
    step = size if size <= 960 else size // 2
    for m in range(0, size, step):
        for n in range(0, out.shape[1], 512):
            value = dot_nt(grads[first + m : first + m + step, :], weights[n : n + 512, :])
            out[place + m : place + m + step, n : n + 512] = value.astype(BF)


def load_pair(copies, wgate, wup, block, target):
    hidden = wgate.shape[1]
    return [copies.start(wgate.at[block], target.at[:, :hidden]), copies.start(wup.at[block], target.at[:, hidden:])]


def far_kernel(info, acc, far_a, far_b, down, fgate, fup, wgate, wup, out_a, out_b, grads,
               xs, ws, sums, factors, gs, outs, sems):
    _, rows, narrow = far_a.shape
    far, to = (far_a, far_b), (out_a, out_b)

    def run(core):
        copies = Copies(sems)
        columns = range(4) if core == 0 else (FAR,)
        load_sum = copies.start(acc, sums)
        steps = []
        order = range(4) if core == 0 else SIDES + (FAR,)
        loads = []
        for n, i1 in enumerate(order):
            loads.append([])
            if n < len(columns):
                loads[n].append(copies.start(down.at[:, block_at(info, columns[n], narrow)], ws.at[n]))
            loads[n].append(copies.start(far[i1 // 2].at[i1 % 2], xs.at[pl.ds(n * rows, rows)]))
        load_factors = [copies.start(fgate, factors.at[0]), copies.start(fup, factors.at[1])]
        weights = []
        for n, column in enumerate(columns):
            block = block_at(info, column, narrow)
            weights.append(load_pair(copies, wgate, wup, block, gs.at[n]))
        load_sum.wait()
        if core == 1:
            for copy in sum(loads, []):
                copy.wait()
        else:
            value = sums[3 * rows :, :]
            for n in range(4):
                for copy in loads[n]:
                    copy.wait()
                value = value + dot_nt(xs[n * rows : (n + 1) * rows, :], ws[n])
            sums[3 * rows :, :] = value
        if core == 1:
            sums[...] += dot_nt(xs[...], ws[0])
        for copy in load_factors:
            copy.wait()
        hidden = sums.shape[1]
        grads[:, :hidden] = (sums[...] * factors[0].astype(F32)).astype(BF)
        grads[:, hidden:] = (sums[...] * factors[1].astype(F32)).astype(BF)
        stores = []
        for n in range(len(columns)):
            for copy in weights[n]:
                copy.wait()
            if core == 0:
                product(grads, 3 * rows, rows, gs.at[n], outs, n * rows)
                parts = [(n, n)]
            else:
                product(grads, 0, 4 * rows, gs.at[n], outs, 0)
                parts = list(enumerate(order))
            for place, i1 in parts:
                stores.append(copies.start(outs.at[pl.ds(place * rows, rows)], to[i1 // 2].at[i1 % 2]))
        for copy in stores:
            copy.wait()

    by_core(info, run)


def far_part(info, acc, far_a, far_b, w_down, factor_gate, factor_up, w_gate, w_up, name):
    _, rows, narrow = far_a.shape
    hidden = w_down.shape[0]
    return pl.pallas_call(
        far_kernel,
        in_specs=[IN_SMEM] + [ANY] * 8,
        out_specs=[ANY, ANY, IN_VMEM],
        out_shape=[
            jax.ShapeDtypeStruct((2, rows, narrow), BF),
            jax.ShapeDtypeStruct((2, rows, narrow), BF),
            jax.ShapeDtypeStruct((4 * rows, 2 * hidden), BF),
        ],
        scratch_shapes=[
            pltpu.VMEM((4 * rows, narrow), BF),
            pltpu.VMEM((4, hidden, narrow), BF),
            pltpu.VMEM((4 * rows, hidden), F32),
            pltpu.VMEM((2, 4 * rows, hidden), BF),
            pltpu.VMEM((4, narrow, 2 * hidden), BF),
            pltpu.VMEM((4 * rows, narrow), BF),
            pltpu.SemaphoreType.DMA((24,)),
        ],
        compiler_params=pltpu.CompilerParams(vmem_limit_bytes=VMEM),
        cost_estimate=pl.CostEstimate(
            flops=24 * rows * narrow * hidden,
            bytes_accessed=16 * rows * narrow + 6 * w_down.size + 64 * rows * hidden,
            transcendentals=0,
        ),
        name=name,
    )(info, acc, far_a, far_b, w_down, factor_gate, factor_up, w_gate, w_up)


def sides_kernel(info, grads, wgate, wup, *refs):
    pieces, (gs, outs, sems) = refs[:6], refs[6:]
    _, rows, narrow = pieces[0].shape

    def run(core):
        copies = Copies(sems)
        columns = range(4) if core == 0 else SIDES
        weights, stores = [], []
        for n, column in enumerate(columns):
            block = block_at(info, column, narrow)
            weights.append(load_pair(copies, wgate, wup, block, gs.at[n]))
        for n in range(len(columns)):
            for copy in weights[n]:
                copy.wait()
            parts = [(s, n) for s in range(3)] if core == 0 else [(n, i1) for i1 in SIDES + (FAR,)]
            first, size = n * len(parts) * rows, len(parts) * rows
            product(grads, 0, size, gs.at[n], outs, first)
            for m, (s, i1) in enumerate(parts):
                stores.append(
                    copies.start(outs.at[pl.ds(first + m * rows, rows)], pieces[2 * s + i1 // 2].at[i1 % 2])
                )
        for copy in stores:
            copy.wait()

    by_core(info, run)


def sides_part(info, grads, w_gate, w_up, name):
    rows, hidden = grads.shape[0] // 4, w_gate.shape[1]
    narrow = w_gate.shape[0] // RING
    return pl.pallas_call(
        sides_kernel,
        in_specs=[IN_SMEM, IN_VMEM, ANY, ANY],
        out_specs=[ANY] * 6,
        out_shape=[jax.ShapeDtypeStruct((2, rows, narrow), BF)] * 6,
        scratch_shapes=[
            pltpu.VMEM((4, narrow, 2 * hidden), BF),
            pltpu.VMEM((12 * rows, narrow), BF),
            pltpu.SemaphoreType.DMA((20,)),
        ],
        compiler_params=pltpu.CompilerParams(vmem_limit_bytes=VMEM),
        cost_estimate=pl.CostEstimate(
            flops=48 * rows * narrow * hidden,
            bytes_accessed=24 * rows * narrow + 4 * w_gate.size,
            transcendentals=0,
        ),
        name=name,
    )(info, grads, w_gate, w_up)


def relative_order(array, x, core, row):
    array = array.reshape((4, 4, 2) + array.shape[2:])
    array = lax.dynamic_slice_in_dim(jnp.concatenate([array, array], axis=0), row, 4, axis=0)
    array = lax.dynamic_slice_in_dim(jnp.concatenate([array, array], axis=1), x, 4, axis=1)
    array = jnp.stack([array[n] for n in SIDES + (FAR,)])
    return jnp.where(core == 0, array, array[:, :, ::-1])


def gather_small(rows):
    return [
        rows,
        receive_from(rows, 0, 1),
        receive_from(rows, 0, 2),
        receive_from(rows, 0, 3),
    ]


def body(grad_out, routes, combine, w_gate, w_up, w_down, stash_gate, stash_up, stash_scale):
    exp = lax.axis_index("exp")
    row = lax.axis_index("row")
    col = lax.axis_index("col")
    x, core = exp // 2, exp % 2
    w_gate, w_up, w_down = w_gate[0], w_up[0], w_down[0]
    capacity = stash_gate.shape[3]
    tokens, narrow = grad_out.shape
    hidden = w_gate.shape[1]

    flat = routes.reshape(-1)
    onehot = (flat[:, None] == jnp.arange(8, dtype=jnp.int32)[None, :]).astype(jnp.int32)
    before = jnp.cumsum(onehot, axis=0) - onehot
    slot_index = jnp.sum(before * onehot, axis=1)
    place = ((flat % 2) ^ core) * 4 + (x - flat // 2) % 4
    target = place * capacity + slot_index
    matches = jnp.arange(8 * capacity, dtype=jnp.int32)[:, None] == target[None, :]
    matches = matches.reshape(8 * capacity, tokens, 2)
    picker = jnp.any(matches, axis=2).astype(BF)
    weight = jnp.sum(jnp.where(matches, combine[None, :, :], 0.0), axis=(1, 2))
    copied = jnp.dot(picker, grad_out, preferred_element_type=F32)
    slots = (copied * weight[:, None]).astype(BF).reshape(2, 4, capacity, narrow)

    other = swap_cores(slots[1])
    held = jnp.stack([slots[0], other], axis=1)
    near = held[0].reshape(2 * capacity, narrow)
    arrived = [receive_along_x(held[j], j) for j in (1, 3, 2)]

    stash = [relative_order(array[:, :, 0], x, core, row) for array in (stash_gate, stash_up)]
    scale = [relative_order(stash_scale[n, :, :, 0], x, core, row) for n in range(2)]

    def factors_of(part):
        gate_pre = stash[0][:, part].astype(F32) * scale[0][:, part, ..., None]
        up_pre = stash[1][:, part].astype(F32) * scale[1][:, part, ..., None]
        sigmoid_gate = jax.nn.sigmoid(gate_pre)
        factor_up = gate_pre * sigmoid_gate
        factor_gate = up_pre * sigmoid_gate * (1.0 + gate_pre * (1.0 - sigmoid_gate))
        return factor_gate.reshape(-1, hidden).astype(BF), factor_up.reshape(-1, hidden).astype(BF)

    factors = factors_of(slice(0, 4))
    info = jnp.stack([core, col]).astype(jnp.int32)

    def gather_near(small):
        own_a, own_b = jnp.stack(small[:2]), jnp.stack(small[2:])
        plus_a, minus_b = receive_from(own_a, 1, 1), receive_from(own_b, 1, 3)
        plus_b, minus_a = receive_from(own_b, 1, 1), receive_from(own_a, 1, 3)
        return own_a, own_b, plus_a, plus_b, minus_a, minus_b

    def gather_far(plus_a, minus_b):
        return receive_from(plus_a, 1, 1), receive_from(minus_b, 1, 3)

    near_small = gather_small(near)
    rest = jnp.stack([arrived[0], arrived[2], arrived[1]]).reshape(6 * capacity, narrow)
    rest_small = gather_small(after(rest, *near_small))
    pieces = gather_near([jnp.concatenate(pair) for pair in zip(near_small, rest_small)])
    far = gather_far(pieces[2], pieces[5])
    acc = hidden_part(info, pieces, w_down, "hidden_sides")
    out = far_part(info, acc, *far, w_down, *factors, w_gate, w_up, "hidden_far")

    def scatter_far(out_a, out_b):
        return receive_from(out_a, 1, 3), receive_from(out_b, 1, 1)

    def add(a, b):
        return (a.astype(F32) + b.astype(F32)).astype(BF)

    def scatter_free(plus_b, minus_a):
        return receive_from(plus_b, 1, 3), receive_from(minus_a, 1, 1)

    def scatter_late(terms, got, free):
        own_a, own_b, plus_a, _, _, minus_b = terms
        back_b, ahead_a = free
        back_a, ahead_b = receive_from(add(plus_a, got[0]), 1, 3), receive_from(add(minus_b, got[1]), 1, 1)
        parts = ((own_a, back_a, ahead_a), (own_b, back_b, ahead_b))

        def total(n, rows):
            return sum(part[n % 2, rows].astype(F32) for part in parts[n // 2]).astype(BF)

        return total

    def scatter_small(total):
        got = [receive_from(total[1], 0, 3), receive_from(total[2], 0, 2), receive_from(total[3], 0, 1)]
        summed = total[0].astype(F32)
        for part in got:
            summed = summed + part.astype(F32)
        return summed.astype(BF)

    got = scatter_far(out[0], out[1])
    terms = sides_part(info, out[2], w_gate, w_up, "terms_sides")
    half = scatter_free(terms[3], terms[4])
    got = lax.optimization_barrier((*got, *terms))[:2]
    total = scatter_late(terms, got, half)
    near_rows, rest_rows = slice(0, 2 * capacity), slice(2 * capacity, 8 * capacity)
    rest_sum = scatter_small([total(n, rest_rows) for n in range(4)]).reshape(3, 2, capacity, narrow)
    near_sum = scatter_small([total(n, near_rows) for n in range(4)]).reshape(1, 2, capacity, narrow)

    back = jnp.stack([receive_along_x(rest_sum[j - 1], -j) for j in (1, 2, 3)])
    returned = jnp.concatenate(
        [near_sum[:, 0], back[:, 0], swap_cores(near_sum[:, 1]), swap_cores(back[:, 1])], axis=0
    ).reshape(8 * capacity, narrow)
    result = lax.dot_general(picker, returned, (((0,), (0,)), ((), ())), preferred_element_type=F32)
    return result.astype(BF)


def solution(mesh):
    placed = (
        P(("exp", "row"), "col"),
        P(("exp", "row"), None),
        P(("exp", "row"), None),
        P("exp", None, ("row", "col")),
        P("exp", None, ("row", "col")),
        P("exp", ("row", "col"), None),
        P(None, None, "exp", None, ("row", "col")),
        P(None, None, "exp", None, ("row", "col")),
        P(None, None, None, "exp", None),
    )
    return jax.shard_map(
        body, mesh=mesh, in_specs=placed, out_specs=P(("exp", "row"), "col"), check_vma=False
    )
```

```python
import functools

import jax
import jax.numpy as jnp
from jax import lax
from jax.experimental import pallas as pl
from jax.experimental.pallas import tpu as pltpu
from jax.sharding import PartitionSpec as P

ALL = ("exp", "row", "col")
BF = jnp.bfloat16
F32 = jnp.float32
RING = 4
VMEM = 60 * 1024 * 1024


def all_devices():
    for x in range(4):
        for k in range(2):
            for z in range(4):
                for y in range(4):
                    yield x, k, z, y


def device_id(x, k, z, y):
    return (((x % 4) * 2 + k) * 4 + z % 4) * 4 + y % 4


def receive_from(value, stage, offset):
    pairs = []
    for x, k, z, y in all_devices():
        if k == stage:
            source = device_id(x, k, z, y + offset)
        else:
            source = device_id(x, k, z + offset, y)
        pairs.append((source, device_id(x, k, z, y)))
    return lax.ppermute(value, ALL, pairs)


def receive_along_x(value, offset):
    pairs = [(device_id(x + offset, k, z, y), device_id(x, k, z, y)) for x, k, z, y in all_devices()]
    return lax.ppermute(value, ALL, pairs)


def swap_cores(value):
    pairs = [(device_id(x, 1 - k, z, y), device_id(x, k, z, y)) for x, k, z, y in all_devices()]
    return lax.ppermute(value, ALL, pairs)


def dot_nt(a, b):
    return lax.dot_general(a, b, (((1,), (1,)), ((), ())), preferred_element_type=F32)


def after(value, *others):
    return lax.optimization_barrier((value, *others))[0]


SIDES = (0, 1, 3)
FAR = 2
ANY = pl.BlockSpec(memory_space=pl.ANY)
IN_VMEM = pl.BlockSpec(memory_space=pltpu.VMEM)
IN_SMEM = pl.BlockSpec(memory_space=pltpu.SMEM)


class Copies:
    def __init__(self, sems):
        self.sems, self.used = sems, 0

    def start(self, source, target):
        copy = pltpu.make_async_copy(source, target, self.sems.at[self.used])
        self.used += 1
        copy.start()
        return copy


def block_at(info, offset, narrow):
    return pl.ds(pl.multiple_of(lax.rem(info[1] + offset, RING) * narrow, 128), narrow)


def by_core(info, run):
    for core in range(2):

        @pl.when(info[0] == core)
        def _():
            run(core)


def hidden_kernel(info, *refs):
    pieces, (down, acc, xs, ws, sems) = refs[:6], refs[6:]
    _, rows, narrow = pieces[0].shape

    def run(core):
        copies = Copies(sems)
        steps = []
        for step in range(4 if core == 0 else 3):
            column = step if core == 0 else SIDES[step]
            waits = [copies.start(down.at[:, block_at(info, column, narrow)], ws.at[step])]
            parts = [(s, step) for s in range(3)] if core == 0 else [(step, i1) for i1 in SIDES + (FAR,)]
            first = step * len(parts)
            for n, (s, i1) in enumerate(parts):
                waits.append(
                    copies.start(pieces[2 * s + i1 // 2].at[i1 % 2], xs.at[pl.ds((first + n) * rows, rows)])
                )
            steps.append((step, first * rows, len(parts) * rows, waits))
        for step, first, size, waits in steps:
            for copy in waits:
                copy.wait()
            value = dot_nt(xs[first : first + size, :], ws[step])
            if step == 0:
                acc[:size, :] = value
            else:
                acc[:size, :] += value
        if core == 0:
            acc[3 * rows :, :] = jnp.zeros((rows, acc.shape[1]), F32)

    by_core(info, run)


def hidden_part(info, pieces, w_down, name):
    _, rows, narrow = pieces[0].shape
    hidden = w_down.shape[0]
    return pl.pallas_call(
        hidden_kernel,
        in_specs=[IN_SMEM] + [ANY] * 7,
        out_specs=IN_VMEM,
        out_shape=jax.ShapeDtypeStruct((4 * rows, hidden), F32),
        scratch_shapes=[
            pltpu.VMEM((12 * rows, narrow), BF),
            pltpu.VMEM((4, hidden, narrow), BF),
            pltpu.SemaphoreType.DMA((16,)),
        ],
        compiler_params=pltpu.CompilerParams(vmem_limit_bytes=VMEM),
        cost_estimate=pl.CostEstimate(
            flops=24 * rows * narrow * hidden,
            bytes_accessed=24 * rows * narrow + 2 * w_down.size + 16 * rows * hidden,
            transcendentals=0,
        ),
        name=name,
    )(info, *pieces, w_down)


def product(grads, first, size, weights, out, place):
    step = size if size <= 960 else size // 2
    for m in range(0, size, step):
        for n in range(0, out.shape[1], 512):
            value = dot_nt(grads[first + m : first + m + step, :], weights[n : n + 512, :])
            out[place + m : place + m + step, n : n + 512] = value.astype(BF)


def load_pair(copies, wgate, wup, block, target):
    hidden = wgate.shape[1]
    return [copies.start(wgate.at[block], target.at[:, :hidden]), copies.start(wup.at[block], target.at[:, hidden:])]


def far_kernel(info, acc, far_a, far_b, down, fgate, fup, wgate, wup, out_a, out_b, grads,
               xs, ws, sums, factors, gs, outs, sems):
    _, rows, narrow = far_a.shape
    far, to = (far_a, far_b), (out_a, out_b)

    def run(core):
        copies = Copies(sems)
        columns = range(4) if core == 0 else (FAR,)
        load_sum = copies.start(acc, sums)
        steps = []
        order = range(4) if core == 0 else SIDES + (FAR,)
        loads = []
        for n, i1 in enumerate(order):
            loads.append([])
            if n < len(columns):
                loads[n].append(copies.start(down.at[:, block_at(info, columns[n], narrow)], ws.at[n]))
            loads[n].append(copies.start(far[i1 // 2].at[i1 % 2], xs.at[pl.ds(n * rows, rows)]))
        load_factors = [copies.start(fgate, factors.at[0]), copies.start(fup, factors.at[1])]
        weights = []
        for n, column in enumerate(columns):
            block = block_at(info, column, narrow)
            weights.append(load_pair(copies, wgate, wup, block, gs.at[n]))
        load_sum.wait()
        if core == 1:
            for copy in sum(loads, []):
                copy.wait()
        else:
            value = sums[3 * rows :, :]
            for n in range(4):
                for copy in loads[n]:
                    copy.wait()
                value = value + dot_nt(xs[n * rows : (n + 1) * rows, :], ws[n])
            sums[3 * rows :, :] = value
        if core == 1:
            sums[...] += dot_nt(xs[...], ws[0])
        for copy in load_factors:
            copy.wait()
        hidden = sums.shape[1]
        grads[:, :hidden] = (sums[...] * factors[0].astype(F32)).astype(BF)
        grads[:, hidden:] = (sums[...] * factors[1].astype(F32)).astype(BF)
        stores = []
        for n in range(len(columns)):
            for copy in weights[n]:
                copy.wait()
            if core == 0:
                product(grads, 3 * rows, rows, gs.at[n], outs, n * rows)
                parts = [(n, n)]
            else:
                product(grads, 0, 4 * rows, gs.at[n], outs, 0)
                parts = list(enumerate(order))
            for place, i1 in parts:
                stores.append(copies.start(outs.at[pl.ds(place * rows, rows)], to[i1 // 2].at[i1 % 2]))
        for copy in stores:
            copy.wait()

    by_core(info, run)


def far_part(info, acc, far_a, far_b, w_down, factor_gate, factor_up, w_gate, w_up, name):
    _, rows, narrow = far_a.shape
    hidden = w_down.shape[0]
    return pl.pallas_call(
        far_kernel,
        in_specs=[IN_SMEM] + [ANY] * 8,
        out_specs=[ANY, ANY, IN_VMEM],
        out_shape=[
            jax.ShapeDtypeStruct((2, rows, narrow), BF),
            jax.ShapeDtypeStruct((2, rows, narrow), BF),
            jax.ShapeDtypeStruct((4 * rows, 2 * hidden), BF),
        ],
        scratch_shapes=[
            pltpu.VMEM((4 * rows, narrow), BF),
            pltpu.VMEM((4, hidden, narrow), BF),
            pltpu.VMEM((4 * rows, hidden), F32),
            pltpu.VMEM((2, 4 * rows, hidden), BF),
            pltpu.VMEM((4, narrow, 2 * hidden), BF),
            pltpu.VMEM((4 * rows, narrow), BF),
            pltpu.SemaphoreType.DMA((24,)),
        ],
        compiler_params=pltpu.CompilerParams(vmem_limit_bytes=VMEM),
        cost_estimate=pl.CostEstimate(
            flops=24 * rows * narrow * hidden,
            bytes_accessed=16 * rows * narrow + 6 * w_down.size + 64 * rows * hidden,
            transcendentals=0,
        ),
        name=name,
    )(info, acc, far_a, far_b, w_down, factor_gate, factor_up, w_gate, w_up)


def sides_kernel(info, grads, wgate, wup, *refs):
    pieces, (gs, outs, sems) = refs[:6], refs[6:]
    _, rows, narrow = pieces[0].shape

    def run(core):
        copies = Copies(sems)
        columns = range(4) if core == 0 else SIDES
        weights, stores = [], []
        for n, column in enumerate(columns):
            block = block_at(info, column, narrow)
            weights.append(load_pair(copies, wgate, wup, block, gs.at[n]))
        for n in range(len(columns)):
            for copy in weights[n]:
                copy.wait()
            parts = [(s, n) for s in range(3)] if core == 0 else [(n, i1) for i1 in SIDES + (FAR,)]
            first, size = n * len(parts) * rows, len(parts) * rows
            product(grads, 0, size, gs.at[n], outs, first)
            for m, (s, i1) in enumerate(parts):
                stores.append(
                    copies.start(outs.at[pl.ds(first + m * rows, rows)], pieces[2 * s + i1 // 2].at[i1 % 2])
                )
        for copy in stores:
            copy.wait()

    by_core(info, run)


def sides_part(info, grads, w_gate, w_up, name):
    rows, hidden = grads.shape[0] // 4, w_gate.shape[1]
    narrow = w_gate.shape[0] // RING
    return pl.pallas_call(
        sides_kernel,
        in_specs=[IN_SMEM, IN_VMEM, ANY, ANY],
        out_specs=[ANY] * 6,
        out_shape=[jax.ShapeDtypeStruct((2, rows, narrow), BF)] * 6,
        scratch_shapes=[
            pltpu.VMEM((4, narrow, 2 * hidden), BF),
            pltpu.VMEM((12 * rows, narrow), BF),
            pltpu.SemaphoreType.DMA((20,)),
        ],
        compiler_params=pltpu.CompilerParams(vmem_limit_bytes=VMEM),
        cost_estimate=pl.CostEstimate(
            flops=48 * rows * narrow * hidden,
            bytes_accessed=24 * rows * narrow + 4 * w_gate.size,
            transcendentals=0,
        ),
        name=name,
    )(info, grads, w_gate, w_up)


def relative_order(array, x, core, row):
    array = array.reshape((4, 4, 2) + array.shape[2:])
    array = lax.dynamic_slice_in_dim(jnp.concatenate([array, array], axis=0), row, 4, axis=0)
    array = lax.dynamic_slice_in_dim(jnp.concatenate([array, array], axis=1), x, 4, axis=1)
    array = jnp.stack([array[n] for n in SIDES + (FAR,)])
    array = jnp.stack([array[:, n] for n in (0, 2, 1, 3)], axis=1)
    return jnp.where(core == 0, array, array[:, :, ::-1])


def gather_small(rows):
    return [
        rows,
        receive_from(rows, 0, 1),
        receive_from(rows, 0, 2),
        receive_from(rows, 0, 3),
    ]


def body(grad_out, routes, combine, w_gate, w_up, w_down, stash_gate, stash_up, stash_scale):
    exp = lax.axis_index("exp")
    row = lax.axis_index("row")
    col = lax.axis_index("col")
    x, core = exp // 2, exp % 2
    w_gate, w_up, w_down = w_gate[0], w_up[0], w_down[0]
    capacity = stash_gate.shape[3]
    tokens, narrow = grad_out.shape
    hidden = w_gate.shape[1]

    flat = routes.reshape(-1)
    onehot = (flat[:, None] == jnp.arange(8, dtype=jnp.int32)[None, :]).astype(jnp.int32)
    before = jnp.cumsum(onehot, axis=0) - onehot
    slot_index = jnp.sum(before * onehot, axis=1)
    place = ((flat % 2) ^ core) * 4 + (x - flat // 2) % 4
    target = place * capacity + slot_index
    matches = jnp.arange(8 * capacity, dtype=jnp.int32)[:, None] == target[None, :]
    matches = matches.reshape(8 * capacity, tokens, 2)
    picker = jnp.any(matches, axis=2).astype(BF)
    weight = jnp.sum(jnp.where(matches, combine[None, :, :], 0.0), axis=(1, 2))
    copied = jnp.dot(picker, grad_out, preferred_element_type=F32)
    slots = (copied * weight[:, None]).astype(BF).reshape(2, 4, capacity, narrow)

    other = swap_cores(slots[1])
    held = jnp.stack([slots[0], other], axis=1)
    near = held[0].reshape(2 * capacity, narrow)
    arrived = [receive_along_x(held[j], j) for j in (1, 3, 2)]

    near_small = gather_small(near)
    stash_gate, stash_up, stash_scale, *_ = lax.optimization_barrier(
        (stash_gate, stash_up, stash_scale, near_small[1])
    )
    stash = [relative_order(array[:, :, 0], x, core, row) for array in (stash_gate, stash_up)]
    scale = [relative_order(stash_scale[n, :, :, 0], x, core, row) for n in range(2)]

    def factors_of(part):
        gate_pre = stash[0][:, part].astype(F32) * scale[0][:, part, ..., None]
        up_pre = stash[1][:, part].astype(F32) * scale[1][:, part, ..., None]
        sigmoid_gate = jax.nn.sigmoid(gate_pre)
        factor_up = gate_pre * sigmoid_gate
        factor_gate = up_pre * sigmoid_gate * (1.0 + gate_pre * (1.0 - sigmoid_gate))
        return factor_gate.reshape(-1, hidden).astype(BF), factor_up.reshape(-1, hidden).astype(BF)

    factors = factors_of(slice(0, 4))
    info = jnp.stack([core, col]).astype(jnp.int32)

    def gather_near(small):
        own_a, own_b = jnp.stack(small[:2]), jnp.stack(small[2:])
        plus_a, minus_b = receive_from(own_a, 1, 1), receive_from(own_b, 1, 3)
        plus_b, minus_a = receive_from(own_b, 1, 1), receive_from(own_a, 1, 3)
        return own_a, own_b, plus_a, plus_b, minus_a, minus_b

    def gather_far(plus_a, minus_b):
        return receive_from(plus_a, 1, 1), receive_from(minus_b, 1, 3)

    rest = jnp.stack([arrived[2], arrived[0], arrived[1]]).reshape(6 * capacity, narrow)
    rest_small = gather_small(after(rest, *near_small))
    pieces = gather_near([jnp.concatenate(pair) for pair in zip(near_small, rest_small)])
    far = gather_far(pieces[2], pieces[5])
    acc = hidden_part(info, pieces, w_down, "hidden_sides")
    out = far_part(info, acc, *far, w_down, *factors, w_gate, w_up, "hidden_far")

    def scatter_far(out_a, out_b):
        return receive_from(out_a, 1, 3), receive_from(out_b, 1, 1)

    def add(a, b):
        return (a.astype(F32) + b.astype(F32)).astype(BF)

    def scatter_free(plus_b, minus_a):
        return receive_from(plus_b, 1, 3), receive_from(minus_a, 1, 1)

    def scatter_late(terms, got, free):
        own_a, own_b, plus_a, _, _, minus_b = terms
        back_b, ahead_a = free
        back_a, ahead_b = receive_from(add(plus_a, got[0]), 1, 3), receive_from(add(minus_b, got[1]), 1, 1)
        parts = ((own_a, back_a, ahead_a), (own_b, back_b, ahead_b))

        def total(n, rows):
            return sum(part[n % 2, rows].astype(F32) for part in parts[n // 2]).astype(BF)

        return total

    def parts_small(total):
        return [
            total[0],
            receive_from(total[1], 0, 3),
            receive_from(total[2], 0, 2),
            receive_from(total[3], 0, 1),
        ]

    def sum_small(own, got):
        summed = own.astype(F32)
        for part in got:
            summed = summed + part.astype(F32)
        return summed.astype(BF)

    def scatter_small(total):
        own, *got = parts_small(total)
        return sum_small(own, got)

    got = scatter_far(out[0], out[1])
    terms = sides_part(info, out[2], w_gate, w_up, "terms_sides")
    half = scatter_free(terms[3], terms[4])
    got = lax.optimization_barrier((*got, *terms))[:2]
    total = scatter_late(terms, got, half)
    first_rows, second_rows = slice(4 * capacity, 8 * capacity), slice(0, 4 * capacity)
    sides_sum = scatter_small([total(n, first_rows) for n in range(4)]).reshape(2, 2, capacity, narrow)
    back = jnp.stack([receive_along_x(sides_sum[0], -1), receive_along_x(sides_sum[1], -3)])
    other_own, *other_got = parts_small([total(n, second_rows) for n in range(4)])
    other_own, back = lax.optimization_barrier((other_own, back))
    other_sum = sum_small(other_own, other_got).reshape(2, 2, capacity, narrow)
    swapped = swap_cores(back[:, 1])
    opposite = receive_along_x(other_sum[1], -2)
    returned = jnp.concatenate(
        [
            other_sum[:1, 0], back[:1, 0], opposite[None, 0], back[1:, 0],
            swap_cores(other_sum[:1, 1]), swapped[:1], swap_cores(opposite[None, 1]), swapped[1:],
        ],
        axis=0,
    ).reshape(8 * capacity, narrow)
    result = lax.dot_general(picker, returned, (((0,), (0,)), ((), ())), preferred_element_type=F32)
    return result.astype(BF)


def solution(mesh):
    placed = (
        P(("exp", "row"), "col"),
        P(("exp", "row"), None),
        P(("exp", "row"), None),
        P("exp", None, ("row", "col")),
        P("exp", None, ("row", "col")),
        P("exp", ("row", "col"), None),
        P(None, None, "exp", None, ("row", "col")),
        P(None, None, "exp", None, ("row", "col")),
        P(None, None, None, "exp", None),
    )
    return jax.shard_map(
        body, mesh=mesh, in_specs=placed, out_specs=P(("exp", "row"), "col"), check_vma=False
    )
```

```python
import functools

import jax
import jax.numpy as jnp
from jax import lax
from jax.experimental import pallas as pl
from jax.experimental.pallas import tpu as pltpu
from jax.sharding import PartitionSpec as P

ALL = ("exp", "row", "col")
BF = jnp.bfloat16
F32 = jnp.float32
RING = 4
VMEM = 60 * 1024 * 1024


def all_devices():
    for x in range(4):
        for k in range(2):
            for z in range(4):
                for y in range(4):
                    yield x, k, z, y


def device_id(x, k, z, y):
    return (((x % 4) * 2 + k) * 4 + z % 4) * 4 + y % 4


def receive_from(value, stage, offset):
    pairs = []
    for x, k, z, y in all_devices():
        if k == stage:
            source = device_id(x, k, z, y + offset)
        else:
            source = device_id(x, k, z + offset, y)
        pairs.append((source, device_id(x, k, z, y)))
    return lax.ppermute(value, ALL, pairs)


def receive_along_x(value, offset):
    pairs = [(device_id(x + offset, k, z, y), device_id(x, k, z, y)) for x, k, z, y in all_devices()]
    return lax.ppermute(value, ALL, pairs)


def swap_cores(value):
    pairs = [(device_id(x, 1 - k, z, y), device_id(x, k, z, y)) for x, k, z, y in all_devices()]
    return lax.ppermute(value, ALL, pairs)


def dot_nt(a, b):
    return lax.dot_general(a, b, (((1,), (1,)), ((), ())), preferred_element_type=F32)


def after(value, *others):
    return lax.optimization_barrier((value, *others))[0]


SIDES = (0, 1, 3)
FAR = 2
ANY = pl.BlockSpec(memory_space=pl.ANY)
IN_VMEM = pl.BlockSpec(memory_space=pltpu.VMEM)
IN_SMEM = pl.BlockSpec(memory_space=pltpu.SMEM)


class Copies:
    def __init__(self, sems):
        self.sems, self.used = sems, 0

    def start(self, source, target):
        copy = pltpu.make_async_copy(source, target, self.sems.at[self.used])
        self.used += 1
        copy.start()
        return copy


def block_at(info, offset, narrow):
    return pl.ds(pl.multiple_of(lax.rem(info[1] + offset, RING) * narrow, 128), narrow)


def by_core(info, run):
    for core in range(2):

        @pl.when(info[0] == core)
        def _():
            run(core)


def hidden_kernel(info, *refs):
    pieces, (down, acc, xs, ws, sems) = refs[:6], refs[6:]
    _, rows, narrow = pieces[0].shape

    def run(core):
        copies = Copies(sems)
        steps = []
        for step in range(4 if core == 0 else 3):
            column = step if core == 0 else SIDES[step]
            waits = [copies.start(down.at[:, block_at(info, column, narrow)], ws.at[step])]
            parts = [(s, step) for s in range(3)] if core == 0 else [(step, i1) for i1 in SIDES + (FAR,)]
            first = step * len(parts)
            for n, (s, i1) in enumerate(parts):
                waits.append(
                    copies.start(pieces[2 * s + i1 // 2].at[i1 % 2], xs.at[pl.ds((first + n) * rows, rows)])
                )
            steps.append((step, first * rows, len(parts) * rows, waits))
        for step, first, size, waits in steps:
            for copy in waits:
                copy.wait()
            value = dot_nt(xs[first : first + size, :], ws[step])
            if step == 0:
                acc[:size, :] = value
            else:
                acc[:size, :] += value
        if core == 0:
            acc[3 * rows :, :] = jnp.zeros((rows, acc.shape[1]), F32)

    by_core(info, run)


def hidden_part(info, pieces, w_down, name):
    _, rows, narrow = pieces[0].shape
    hidden = w_down.shape[0]
    return pl.pallas_call(
        hidden_kernel,
        in_specs=[IN_SMEM] + [ANY] * 7,
        out_specs=IN_VMEM,
        out_shape=jax.ShapeDtypeStruct((4 * rows, hidden), F32),
        scratch_shapes=[
            pltpu.VMEM((12 * rows, narrow), BF),
            pltpu.VMEM((4, hidden, narrow), BF),
            pltpu.SemaphoreType.DMA((16,)),
        ],
        compiler_params=pltpu.CompilerParams(vmem_limit_bytes=VMEM),
        cost_estimate=pl.CostEstimate(
            flops=24 * rows * narrow * hidden,
            bytes_accessed=24 * rows * narrow + 2 * w_down.size + 16 * rows * hidden,
            transcendentals=0,
        ),
        name=name,
    )(info, *pieces, w_down)


def product(grads, first, size, weights, out, place):
    step = size if size <= 960 else size // 2
    for m in range(0, size, step):
        for n in range(0, out.shape[1], 512):
            value = dot_nt(grads[first + m : first + m + step, :], weights[n : n + 512, :])
            out[place + m : place + m + step, n : n + 512] = value.astype(BF)


def looped_product(grads, size, weights, out, place):
    step = size // 2

    @pl.loop(0, out.shape[1] // 512)
    def _(n):
        columns = pl.ds(pl.multiple_of(n * 512, 512), 512)

        @pl.loop(0, 2)
        def _(m):
            start = pl.multiple_of(m * step, step)
            value = dot_nt(grads[pl.ds(start, step), :], weights[columns, :])
            out[pl.ds(place + start, step), columns] = value.astype(BF)


def load_pair(copies, wgate, wup, block, target):
    hidden = wgate.shape[1]
    return [copies.start(wgate.at[block], target.at[:, :hidden]), copies.start(wup.at[block], target.at[:, hidden:])]


def far_kernel(info, acc, far_a, far_b, down, fgate, fup, wgate, wup, out_a, out_b, grads,
               xs, ws, sums, factors, gs, outs, sems):
    _, rows, narrow = far_a.shape
    far, to = (far_a, far_b), (out_a, out_b)

    def run(core):
        copies = Copies(sems)
        columns = range(4) if core == 0 else (FAR,)
        load_sum = copies.start(acc, sums)
        steps = []
        order = range(4) if core == 0 else SIDES + (FAR,)
        loads = []
        for n, i1 in enumerate(order):
            loads.append([])
            if n < len(columns):
                loads[n].append(copies.start(down.at[:, block_at(info, columns[n], narrow)], ws.at[n]))
            loads[n].append(copies.start(far[i1 // 2].at[i1 % 2], xs.at[pl.ds(n * rows, rows)]))
        load_factors = [copies.start(fgate, factors.at[0]), copies.start(fup, factors.at[1])]
        weights = []
        for n, column in enumerate(columns):
            block = block_at(info, column, narrow)
            weights.append(load_pair(copies, wgate, wup, block, gs.at[n]))
        load_sum.wait()
        if core == 1:
            for copy in sum(loads, []):
                copy.wait()
        else:
            value = sums[3 * rows :, :]
            for n in range(4):
                for copy in loads[n]:
                    copy.wait()
                value = value + dot_nt(xs[n * rows : (n + 1) * rows, :], ws[n])
            sums[3 * rows :, :] = value
        if core == 1:
            sums[...] += dot_nt(xs[...], ws[0])
        for copy in load_factors:
            copy.wait()
        hidden = sums.shape[1]
        grads[:, :hidden] = (sums[...] * factors[0].astype(F32)).astype(BF)
        grads[:, hidden:] = (sums[...] * factors[1].astype(F32)).astype(BF)
        stores = []
        for n in range(len(columns)):
            for copy in weights[n]:
                copy.wait()
            if core == 0:
                product(grads, 3 * rows, rows, gs.at[n], outs, n * rows)
                parts = [(n, n)]
            else:
                product(grads, 0, 4 * rows, gs.at[n], outs, 0)
                parts = list(enumerate(order))
            for place, i1 in parts:
                stores.append(copies.start(outs.at[pl.ds(place * rows, rows)], to[i1 // 2].at[i1 % 2]))
        for copy in stores:
            copy.wait()

    by_core(info, run)


def far_part(info, acc, far_a, far_b, w_down, factor_gate, factor_up, w_gate, w_up, name):
    _, rows, narrow = far_a.shape
    hidden = w_down.shape[0]
    return pl.pallas_call(
        far_kernel,
        in_specs=[IN_SMEM] + [ANY] * 8,
        out_specs=[ANY, ANY, IN_VMEM],
        out_shape=[
            jax.ShapeDtypeStruct((2, rows, narrow), BF),
            jax.ShapeDtypeStruct((2, rows, narrow), BF),
            jax.ShapeDtypeStruct((4 * rows, 2 * hidden), BF),
        ],
        scratch_shapes=[
            pltpu.VMEM((4 * rows, narrow), BF),
            pltpu.VMEM((4, hidden, narrow), BF),
            pltpu.VMEM((4 * rows, hidden), F32),
            pltpu.VMEM((2, 4 * rows, hidden), BF),
            pltpu.VMEM((4, narrow, 2 * hidden), BF),
            pltpu.VMEM((4 * rows, narrow), BF),
            pltpu.SemaphoreType.DMA((24,)),
        ],
        compiler_params=pltpu.CompilerParams(vmem_limit_bytes=VMEM),
        cost_estimate=pl.CostEstimate(
            flops=24 * rows * narrow * hidden,
            bytes_accessed=16 * rows * narrow + 6 * w_down.size + 64 * rows * hidden,
            transcendentals=0,
        ),
        name=name,
    )(info, acc, far_a, far_b, w_down, factor_gate, factor_up, w_gate, w_up)


def sides_kernel(info, grads, wgate, wup, *refs):
    pieces, (gs, outs, sems) = refs[:6], refs[6:]
    _, rows, narrow = pieces[0].shape

    def run(core):
        copies = Copies(sems)
        columns = range(4) if core == 0 else SIDES
        weights, stores = [], []
        for n, column in enumerate(columns):
            block = block_at(info, column, narrow)
            weights.append(load_pair(copies, wgate, wup, block, gs.at[n]))
        for n in range(len(columns)):
            for copy in weights[n]:
                copy.wait()
            parts = [(s, n) for s in range(3)] if core == 0 else [(n, i1) for i1 in SIDES + (FAR,)]
            first, size = n * len(parts) * rows, len(parts) * rows
            if core == 0:
                product(grads, 0, size, gs.at[n], outs, first)
            else:
                looped_product(grads, size, gs.at[n], outs, first)
            for m, (s, i1) in enumerate(parts):
                stores.append(
                    copies.start(outs.at[pl.ds(first + m * rows, rows)], pieces[2 * s + i1 // 2].at[i1 % 2])
                )
        for copy in stores:
            copy.wait()

    by_core(info, run)


def sides_part(info, grads, w_gate, w_up, name):
    rows, hidden = grads.shape[0] // 4, w_gate.shape[1]
    narrow = w_gate.shape[0] // RING
    return pl.pallas_call(
        sides_kernel,
        in_specs=[IN_SMEM, IN_VMEM, ANY, ANY],
        out_specs=[ANY] * 6,
        out_shape=[jax.ShapeDtypeStruct((2, rows, narrow), BF)] * 6,
        scratch_shapes=[
            pltpu.VMEM((4, narrow, 2 * hidden), BF),
            pltpu.VMEM((12 * rows, narrow), BF),
            pltpu.SemaphoreType.DMA((20,)),
        ],
        compiler_params=pltpu.CompilerParams(vmem_limit_bytes=VMEM),
        cost_estimate=pl.CostEstimate(
            flops=48 * rows * narrow * hidden,
            bytes_accessed=24 * rows * narrow + 4 * w_gate.size,
            transcendentals=0,
        ),
        name=name,
    )(info, grads, w_gate, w_up)


def relative_order(array, x, core, row):
    array = array.reshape((4, 4, 2) + array.shape[2:])
    array = lax.dynamic_slice_in_dim(jnp.concatenate([array, array], axis=0), row, 4, axis=0)
    array = lax.dynamic_slice_in_dim(jnp.concatenate([array, array], axis=1), x, 4, axis=1)
    array = jnp.stack([array[n] for n in SIDES + (FAR,)])
    array = jnp.stack([array[:, n] for n in (0, 2, 1, 3)], axis=1)
    return jnp.where(core == 0, array, array[:, :, ::-1])


def gather_small(rows):
    return [
        rows,
        receive_from(rows, 0, 1),
        receive_from(rows, 0, 2),
        receive_from(rows, 0, 3),
    ]


def body(grad_out, routes, combine, w_gate, w_up, w_down, stash_gate, stash_up, stash_scale):
    exp = lax.axis_index("exp")
    row = lax.axis_index("row")
    col = lax.axis_index("col")
    x, core = exp // 2, exp % 2
    w_gate, w_up, w_down = w_gate[0], w_up[0], w_down[0]
    capacity = stash_gate.shape[3]
    tokens, narrow = grad_out.shape
    hidden = w_gate.shape[1]

    flat = routes.reshape(-1)
    onehot = (flat[:, None] == jnp.arange(8, dtype=jnp.int32)[None, :]).astype(jnp.int32)
    before = jnp.cumsum(onehot, axis=0) - onehot
    slot_index = jnp.sum(before * onehot, axis=1)
    place = ((flat % 2) ^ core) * 4 + (x - flat // 2) % 4
    target = place * capacity + slot_index
    matches = jnp.arange(8 * capacity, dtype=jnp.int32)[:, None] == target[None, :]
    matches = matches.reshape(8 * capacity, tokens, 2)
    picker = jnp.any(matches, axis=2).astype(BF)
    weight = jnp.sum(jnp.where(matches, combine[None, :, :], 0.0), axis=(1, 2))
    copied = jnp.dot(picker, grad_out, preferred_element_type=F32)
    slots = (copied * weight[:, None]).astype(BF).reshape(2, 4, capacity, narrow)

    other = swap_cores(slots[1])
    held = jnp.stack([slots[0], other], axis=1)
    near = held[0].reshape(2 * capacity, narrow)
    arrived = [receive_along_x(held[j], j) for j in (1, 3, 2)]

    near_small = gather_small(near)
    stash_gate, stash_up, stash_scale, *_ = lax.optimization_barrier(
        (stash_gate, stash_up, stash_scale, near_small[1])
    )
    stash = [relative_order(array[:, :, 0], x, core, row) for array in (stash_gate, stash_up)]
    scale = [relative_order(stash_scale[n, :, :, 0], x, core, row) for n in range(2)]

    def factors_of(part):
        gate_pre = stash[0][:, part].astype(F32) * scale[0][:, part, ..., None]
        up_pre = stash[1][:, part].astype(F32) * scale[1][:, part, ..., None]
        sigmoid_gate = jax.nn.sigmoid(gate_pre)
        factor_up = gate_pre * sigmoid_gate
        factor_gate = up_pre * sigmoid_gate * (1.0 + gate_pre * (1.0 - sigmoid_gate))
        return factor_gate.reshape(-1, hidden).astype(BF), factor_up.reshape(-1, hidden).astype(BF)

    factors = factors_of(slice(0, 4))
    info = jnp.stack([core, col]).astype(jnp.int32)

    def gather_near(small):
        own_a, own_b = jnp.stack(small[:2]), jnp.stack(small[2:])
        plus_a, minus_b = receive_from(own_a, 1, 1), receive_from(own_b, 1, 3)
        plus_b, minus_a = receive_from(own_b, 1, 1), receive_from(own_a, 1, 3)
        return own_a, own_b, plus_a, plus_b, minus_a, minus_b

    def gather_far(plus_a, minus_b):
        return receive_from(plus_a, 1, 1), receive_from(minus_b, 1, 3)

    rest = jnp.stack([arrived[2], arrived[0], arrived[1]]).reshape(6 * capacity, narrow)
    rest_small = gather_small(after(rest, *near_small))
    pieces = gather_near([jnp.concatenate(pair) for pair in zip(near_small, rest_small)])
    far = gather_far(pieces[2], pieces[5])
    acc = hidden_part(info, pieces, w_down, "hidden_sides")
    out = far_part(info, acc, *far, w_down, *factors, w_gate, w_up, "hidden_far")

    def scatter_far(out_a, out_b):
        return receive_from(out_a, 1, 3), receive_from(out_b, 1, 1)

    def add(a, b):
        return (a.astype(F32) + b.astype(F32)).astype(BF)

    def scatter_free(plus_b, minus_a):
        return receive_from(plus_b, 1, 3), receive_from(minus_a, 1, 1)

    def scatter_late(terms, got, free):
        own_a, own_b, plus_a, _, _, minus_b = terms
        back_b, ahead_a = free
        back_a, ahead_b = receive_from(add(plus_a, got[0]), 1, 3), receive_from(add(minus_b, got[1]), 1, 1)
        parts = ((own_a, back_a, ahead_a), (own_b, back_b, ahead_b))

        def total(n, rows):
            return sum(part[n % 2, rows].astype(F32) for part in parts[n // 2]).astype(BF)

        return total

    def parts_small(total):
        return [
            total[0],
            receive_from(total[1], 0, 3),
            receive_from(total[2], 0, 2),
            receive_from(total[3], 0, 1),
        ]

    def sum_small(own, got):
        summed = own.astype(F32)
        for part in got:
            summed = summed + part.astype(F32)
        return summed.astype(BF)

    def scatter_small(total):
        own, *got = parts_small(total)
        return sum_small(own, got)

    got = scatter_far(out[0], out[1])
    terms = sides_part(info, out[2], w_gate, w_up, "terms_sides")
    half = scatter_free(terms[3], terms[4])
    got = lax.optimization_barrier((*got, *terms))[:2]
    total = scatter_late(terms, got, half)
    first_rows, second_rows = slice(4 * capacity, 8 * capacity), slice(0, 4 * capacity)
    sides_sum = scatter_small([total(n, first_rows) for n in range(4)]).reshape(2, 2, capacity, narrow)
    back = jnp.stack([receive_along_x(sides_sum[0], -1), receive_along_x(sides_sum[1], -3)])
    other_own, *other_got = parts_small([total(n, second_rows) for n in range(4)])
    other_own, back = lax.optimization_barrier((other_own, back))
    other_sum = sum_small(other_own, other_got).reshape(2, 2, capacity, narrow)
    swapped = swap_cores(back[:, 1])
    opposite = receive_along_x(other_sum[1], -2)
    returned = jnp.concatenate(
        [
            other_sum[:1, 0], back[:1, 0], opposite[None, 0], back[1:, 0],
            swap_cores(other_sum[:1, 1]), swapped[:1], swap_cores(opposite[None, 1]), swapped[1:],
        ],
        axis=0,
    ).reshape(8 * capacity, narrow)
    result = lax.dot_general(picker, returned, (((0,), (0,)), ((), ())), preferred_element_type=F32)
    return result.astype(BF)


def solution(mesh):
    placed = (
        P(("exp", "row"), "col"),
        P(("exp", "row"), None),
        P(("exp", "row"), None),
        P("exp", None, ("row", "col")),
        P("exp", None, ("row", "col")),
        P("exp", ("row", "col"), None),
        P(None, None, "exp", None, ("row", "col")),
        P(None, None, "exp", None, ("row", "col")),
        P(None, None, None, "exp", None),
    )
    return jax.shard_map(
        body, mesh=mesh, in_specs=placed, out_specs=P(("exp", "row"), "col"), check_vma=False
    )
```

```python
import functools

import jax
import jax.numpy as jnp
from jax import lax
from jax.experimental import pallas as pl
from jax.experimental.pallas import tpu as pltpu
from jax.sharding import PartitionSpec as P

ALL = ("exp", "row", "col")
BF = jnp.bfloat16
F32 = jnp.float32
RING = 4
VMEM = 60 * 1024 * 1024


def all_devices():
    for x in range(4):
        for k in range(2):
            for z in range(4):
                for y in range(4):
                    yield x, k, z, y


def device_id(x, k, z, y):
    return (((x % 4) * 2 + k) * 4 + z % 4) * 4 + y % 4


def receive_from(value, stage, offset):
    pairs = []
    for x, k, z, y in all_devices():
        if k == stage:
            source = device_id(x, k, z, y + offset)
        else:
            source = device_id(x, k, z + offset, y)
        pairs.append((source, device_id(x, k, z, y)))
    return lax.ppermute(value, ALL, pairs)


def receive_along_x(value, offset):
    pairs = [(device_id(x + offset, k, z, y), device_id(x, k, z, y)) for x, k, z, y in all_devices()]
    return lax.ppermute(value, ALL, pairs)


def swap_cores(value):
    pairs = [(device_id(x, 1 - k, z, y), device_id(x, k, z, y)) for x, k, z, y in all_devices()]
    return lax.ppermute(value, ALL, pairs)


def dot_nt(a, b):
    return lax.dot_general(a, b, (((1,), (1,)), ((), ())), preferred_element_type=F32)


def after(value, *others):
    return lax.optimization_barrier((value, *others))[0]


SIDES = (0, 1, 3)
FAR = 2
ANY = pl.BlockSpec(memory_space=pl.ANY)
IN_VMEM = pl.BlockSpec(memory_space=pltpu.VMEM)
IN_SMEM = pl.BlockSpec(memory_space=pltpu.SMEM)


class Copies:
    def __init__(self, sems):
        self.sems, self.used = sems, 0

    def start(self, source, target):
        copy = pltpu.make_async_copy(source, target, self.sems.at[self.used])
        self.used += 1
        copy.start()
        return copy


def block_at(info, offset, narrow):
    return pl.ds(pl.multiple_of(lax.rem(info[1] + offset, RING) * narrow, 128), narrow)


def by_core(info, run):
    for core in range(2):

        @pl.when(info[0] == core)
        def _():
            run(core)


def hidden_kernel(info, *refs):
    pieces, (down, acc, xs, ws, sems) = refs[:6], refs[6:]
    _, rows, narrow = pieces[0].shape

    def run(core):
        copies = Copies(sems)
        steps = []
        for step in range(4 if core == 0 else 3):
            column = step if core == 0 else SIDES[step]
            waits = [copies.start(down.at[:, block_at(info, column, narrow)], ws.at[step])]
            parts = [(s, step) for s in range(3)] if core == 0 else [(step, i1) for i1 in SIDES + (FAR,)]
            first = step * len(parts)
            for n, (s, i1) in enumerate(parts):
                waits.append(
                    copies.start(pieces[2 * s + i1 // 2].at[i1 % 2], xs.at[pl.ds((first + n) * rows, rows)])
                )
            steps.append((step, first * rows, len(parts) * rows, waits))
        for step, first, size, waits in steps:
            for copy in waits:
                copy.wait()
            value = dot_nt(xs[first : first + size, :], ws[step])
            if step == 0:
                acc[:size, :] = value
            else:
                acc[:size, :] += value
        if core == 0:
            acc[3 * rows :, :] = jnp.zeros((rows, acc.shape[1]), F32)

    by_core(info, run)


def hidden_part(info, pieces, w_down, name):
    _, rows, narrow = pieces[0].shape
    hidden = w_down.shape[0]
    return pl.pallas_call(
        hidden_kernel,
        in_specs=[IN_SMEM] + [ANY] * 7,
        out_specs=IN_VMEM,
        out_shape=jax.ShapeDtypeStruct((4 * rows, hidden), F32),
        scratch_shapes=[
            pltpu.VMEM((12 * rows, narrow), BF),
            pltpu.VMEM((4, hidden, narrow), BF),
            pltpu.SemaphoreType.DMA((16,)),
        ],
        compiler_params=pltpu.CompilerParams(vmem_limit_bytes=VMEM),
        cost_estimate=pl.CostEstimate(
            flops=24 * rows * narrow * hidden,
            bytes_accessed=24 * rows * narrow + 2 * w_down.size + 16 * rows * hidden,
            transcendentals=0,
        ),
        name=name,
    )(info, *pieces, w_down)


def product(grads, first, size, weights, out, place):
    step = size if size <= 960 else size // 2
    for m in range(0, size, step):
        for n in range(0, out.shape[1], 512):
            value = dot_nt(grads[first + m : first + m + step, :], weights[n : n + 512, :])
            out[place + m : place + m + step, n : n + 512] = value.astype(BF)


def looped_product(grads, size, weights, out, place):
    step = size // 2

    @pl.loop(0, out.shape[1] // 512)
    def _(n):
        columns = pl.ds(pl.multiple_of(n * 512, 512), 512)

        @pl.loop(0, 2)
        def _(m):
            start = pl.multiple_of(m * step, step)
            value = dot_nt(grads[pl.ds(start, step), :], weights[columns, :])
            out[pl.ds(place + start, step), columns] = value.astype(BF)


def load_pair(copies, wgate, wup, block, target):
    hidden = wgate.shape[1]
    return [copies.start(wgate.at[block], target.at[:, :hidden]), copies.start(wup.at[block], target.at[:, hidden:])]


def far_kernel(info, acc, far_a, far_b, down, fgate, fup, wgate, wup, out_a, out_b, grads_out,
               xs, ws, sums, factors, gs, outs, grads, sems):
    _, rows, narrow = far_a.shape
    far, to = (far_a, far_b), (out_a, out_b)

    def run(core):
        copies = Copies(sems)
        columns = range(4) if core == 0 else (FAR,)
        load_sum = copies.start(acc, sums)
        steps = []
        order = range(4) if core == 0 else SIDES + (FAR,)
        loads = []
        for n, i1 in enumerate(order):
            loads.append([])
            if n < len(columns):
                loads[n].append(copies.start(down.at[:, block_at(info, columns[n], narrow)], ws.at[n]))
            loads[n].append(copies.start(far[i1 // 2].at[i1 % 2], xs.at[pl.ds(n * rows, rows)]))
        load_factors = [copies.start(fgate, factors.at[0]), copies.start(fup, factors.at[1])]
        weights = []
        for n, column in enumerate(columns):
            block = block_at(info, column, narrow)
            weights.append(load_pair(copies, wgate, wup, block, gs.at[n]))
        load_sum.wait()
        if core == 1:
            for copy in sum(loads, []):
                copy.wait()
        else:
            value = sums[3 * rows :, :]
            for n in range(4):
                for copy in loads[n]:
                    copy.wait()
                value = value + dot_nt(xs[n * rows : (n + 1) * rows, :], ws[n])
            sums[3 * rows :, :] = value
        if core == 1:
            sums[...] += dot_nt(xs[...], ws[0])
        for copy in load_factors:
            copy.wait()
        hidden = sums.shape[1]
        grads[:, :hidden] = (sums[...] * factors[0].astype(F32)).astype(BF)
        grads[:, hidden:] = (sums[...] * factors[1].astype(F32)).astype(BF)
        stores = [copies.start(grads, grads_out)]
        for n in range(len(columns)):
            for copy in weights[n]:
                copy.wait()
            if core == 0:
                product(grads, 3 * rows, rows, gs.at[n], outs, n * rows)
                parts = [(n, n)]
            else:
                product(grads, 0, 4 * rows, gs.at[n], outs, 0)
                parts = list(enumerate(order))
            for place, i1 in parts:
                stores.append(copies.start(outs.at[pl.ds(place * rows, rows)], to[i1 // 2].at[i1 % 2]))
        for copy in stores:
            copy.wait()

    by_core(info, run)


def far_part(info, acc, far_a, far_b, w_down, factor_gate, factor_up, w_gate, w_up, name):
    _, rows, narrow = far_a.shape
    hidden = w_down.shape[0]
    return pl.pallas_call(
        far_kernel,
        in_specs=[IN_SMEM] + [ANY] * 8,
        out_specs=[ANY, ANY, ANY],
        out_shape=[
            jax.ShapeDtypeStruct((2, rows, narrow), BF),
            jax.ShapeDtypeStruct((2, rows, narrow), BF),
            jax.ShapeDtypeStruct((4 * rows, 2 * hidden), BF),
        ],
        scratch_shapes=[
            pltpu.VMEM((4 * rows, narrow), BF),
            pltpu.VMEM((4, hidden, narrow), BF),
            pltpu.VMEM((4 * rows, hidden), F32),
            pltpu.VMEM((2, 4 * rows, hidden), BF),
            pltpu.VMEM((4, narrow, 2 * hidden), BF),
            pltpu.VMEM((4 * rows, narrow), BF),
            pltpu.VMEM((4 * rows, 2 * hidden), BF),
            pltpu.SemaphoreType.DMA((24,)),
        ],
        compiler_params=pltpu.CompilerParams(vmem_limit_bytes=VMEM),
        cost_estimate=pl.CostEstimate(
            flops=24 * rows * narrow * hidden,
            bytes_accessed=16 * rows * narrow + 6 * w_down.size + 64 * rows * hidden,
            transcendentals=0,
        ),
        name=name,
    )(info, acc, far_a, far_b, w_down, factor_gate, factor_up, w_gate, w_up)


def sides_kernel(info, grads, wgate, wup, *refs):
    pieces, (gs, outs, sems) = refs[:6], refs[6:]
    _, rows, narrow = pieces[0].shape

    def run(core):
        copies = Copies(sems)
        columns = range(4) if core == 0 else SIDES
        weights, stores = [], []
        for n, column in enumerate(columns):
            block = block_at(info, column, narrow)
            weights.append(load_pair(copies, wgate, wup, block, gs.at[n]))
        for n in range(len(columns)):
            for copy in weights[n]:
                copy.wait()
            parts = [(s, n) for s in range(3)] if core == 0 else [(n, i1) for i1 in SIDES + (FAR,)]
            first, size = n * len(parts) * rows, len(parts) * rows
            if core == 0:
                product(grads, 0, size, gs.at[n], outs, first)
            else:
                looped_product(grads, size, gs.at[n], outs, first)
            for m, (s, i1) in enumerate(parts):
                stores.append(
                    copies.start(outs.at[pl.ds(first + m * rows, rows)], pieces[2 * s + i1 // 2].at[i1 % 2])
                )
        for copy in stores:
            copy.wait()

    by_core(info, run)


def sides_part(info, grads, w_gate, w_up, name):
    rows, hidden = grads.shape[0] // 4, w_gate.shape[1]
    narrow = w_gate.shape[0] // RING
    return pl.pallas_call(
        sides_kernel,
        in_specs=[IN_SMEM, IN_VMEM, ANY, ANY],
        out_specs=[ANY] * 6,
        out_shape=[jax.ShapeDtypeStruct((2, rows, narrow), BF)] * 6,
        scratch_shapes=[
            pltpu.VMEM((4, narrow, 2 * hidden), BF),
            pltpu.VMEM((12 * rows, narrow), BF),
            pltpu.SemaphoreType.DMA((20,)),
        ],
        compiler_params=pltpu.CompilerParams(vmem_limit_bytes=VMEM),
        cost_estimate=pl.CostEstimate(
            flops=48 * rows * narrow * hidden,
            bytes_accessed=24 * rows * narrow + 4 * w_gate.size,
            transcendentals=0,
        ),
        name=name,
    )(info, grads, w_gate, w_up)


def relative_order(array, x, core, row):
    array = array.reshape((4, 4, 2) + array.shape[2:])
    array = lax.dynamic_slice_in_dim(jnp.concatenate([array, array], axis=0), row, 4, axis=0)
    array = lax.dynamic_slice_in_dim(jnp.concatenate([array, array], axis=1), x, 4, axis=1)
    array = jnp.stack([array[n] for n in SIDES + (FAR,)])
    array = jnp.stack([array[:, n] for n in (0, 2, 1, 3)], axis=1)
    return jnp.where(core == 0, array, array[:, :, ::-1])


def gather_small(rows):
    return [
        rows,
        receive_from(rows, 0, 1),
        receive_from(rows, 0, 2),
        receive_from(rows, 0, 3),
    ]


def body(grad_out, routes, combine, w_gate, w_up, w_down, stash_gate, stash_up, stash_scale):
    exp = lax.axis_index("exp")
    row = lax.axis_index("row")
    col = lax.axis_index("col")
    x, core = exp // 2, exp % 2
    w_gate, w_up, w_down = w_gate[0], w_up[0], w_down[0]
    capacity = stash_gate.shape[3]
    tokens, narrow = grad_out.shape
    hidden = w_gate.shape[1]

    flat = routes.reshape(-1)
    onehot = (flat[:, None] == jnp.arange(8, dtype=jnp.int32)[None, :]).astype(jnp.int32)
    before = jnp.cumsum(onehot, axis=0) - onehot
    slot_index = jnp.sum(before * onehot, axis=1)
    place = ((flat % 2) ^ core) * 4 + (x - flat // 2) % 4
    target = place * capacity + slot_index
    matches = jnp.arange(8 * capacity, dtype=jnp.int32)[:, None] == target[None, :]
    matches = matches.reshape(8 * capacity, tokens, 2)
    picker = jnp.any(matches, axis=2).astype(BF)
    weight = jnp.sum(jnp.where(matches, combine[None, :, :], 0.0), axis=(1, 2))
    copied = jnp.dot(picker, grad_out, preferred_element_type=F32)
    slots = (copied * weight[:, None]).astype(BF).reshape(2, 4, capacity, narrow)

    other = swap_cores(slots[1])
    held = jnp.stack([slots[0], other], axis=1)
    near = held[0].reshape(2 * capacity, narrow)
    arrived = [receive_along_x(held[j], j) for j in (1, 3, 2)]

    near_small = gather_small(near)
    stash_gate, stash_up, stash_scale, *_ = lax.optimization_barrier(
        (stash_gate, stash_up, stash_scale, near_small[1])
    )
    stash = [relative_order(array[:, :, 0], x, core, row) for array in (stash_gate, stash_up)]
    scale = [relative_order(stash_scale[n, :, :, 0], x, core, row) for n in range(2)]

    def factors_of(part):
        gate_pre = stash[0][:, part].astype(F32) * scale[0][:, part, ..., None]
        up_pre = stash[1][:, part].astype(F32) * scale[1][:, part, ..., None]
        sigmoid_gate = jax.nn.sigmoid(gate_pre)
        factor_up = gate_pre * sigmoid_gate
        factor_gate = up_pre * sigmoid_gate * (1.0 + gate_pre * (1.0 - sigmoid_gate))
        return factor_gate.reshape(-1, hidden).astype(BF), factor_up.reshape(-1, hidden).astype(BF)

    factors = factors_of(slice(0, 4))
    info = jnp.stack([core, col]).astype(jnp.int32)

    def gather_near(small):
        own_a, own_b = jnp.stack(small[:2]), jnp.stack(small[2:])
        plus_a, minus_b = receive_from(own_a, 1, 1), receive_from(own_b, 1, 3)
        plus_b, minus_a = receive_from(own_b, 1, 1), receive_from(own_a, 1, 3)
        return own_a, own_b, plus_a, plus_b, minus_a, minus_b

    def gather_far(plus_a, minus_b):
        return receive_from(plus_a, 1, 1), receive_from(minus_b, 1, 3)

    rest = jnp.stack([arrived[2], arrived[0], arrived[1]]).reshape(6 * capacity, narrow)
    rest_small = gather_small(after(rest, *near_small))
    pieces = gather_near([jnp.concatenate(pair) for pair in zip(near_small, rest_small)])
    far = gather_far(pieces[2], pieces[5])
    acc = hidden_part(info, pieces, w_down, "hidden_sides")
    out = far_part(info, acc, *far, w_down, *factors, w_gate, w_up, "hidden_far")

    def scatter_far(out_a, out_b):
        return receive_from(out_a, 1, 3), receive_from(out_b, 1, 1)

    def add(a, b):
        return (a.astype(F32) + b.astype(F32)).astype(BF)

    def scatter_free(plus_b, minus_a):
        return receive_from(plus_b, 1, 3), receive_from(minus_a, 1, 1)

    def scatter_late(terms, got, free):
        own_a, own_b, plus_a, _, _, minus_b = terms
        back_b, ahead_a = free
        back_a, ahead_b = receive_from(add(plus_a, got[0]), 1, 3), receive_from(add(minus_b, got[1]), 1, 1)
        parts = ((own_a, back_a, ahead_a), (own_b, back_b, ahead_b))

        def total(n, rows):
            return sum(part[n % 2, rows].astype(F32) for part in parts[n // 2]).astype(BF)

        return total

    def parts_small(total):
        return [
            total[0],
            receive_from(total[1], 0, 3),
            receive_from(total[2], 0, 2),
            receive_from(total[3], 0, 1),
        ]

    def sum_small(own, got):
        summed = own.astype(F32)
        for part in got:
            summed = summed + part.astype(F32)
        return summed.astype(BF)

    def scatter_small(total):
        own, *got = parts_small(total)
        return sum_small(own, got)

    got = scatter_far(out[0], out[1])
    terms = sides_part(info, out[2], w_gate, w_up, "terms_sides")
    half = scatter_free(terms[3], terms[4])
    got = lax.optimization_barrier((*got, *terms))[:2]
    total = scatter_late(terms, got, half)
    first_rows, second_rows = slice(4 * capacity, 8 * capacity), slice(0, 4 * capacity)
    sides_sum = scatter_small([total(n, first_rows) for n in range(4)]).reshape(2, 2, capacity, narrow)
    back = jnp.stack([receive_along_x(sides_sum[0], -1), receive_along_x(sides_sum[1], -3)])
    other_own, *other_got = parts_small([total(n, second_rows) for n in range(4)])
    other_own, back = lax.optimization_barrier((other_own, back))
    other_sum = sum_small(other_own, other_got).reshape(2, 2, capacity, narrow)
    swapped = swap_cores(back[:, 1])
    opposite = receive_along_x(other_sum[1], -2)
    returned = jnp.concatenate(
        [
            other_sum[:1, 0], back[:1, 0], opposite[None, 0], back[1:, 0],
            swap_cores(other_sum[:1, 1]), swapped[:1], swap_cores(opposite[None, 1]), swapped[1:],
        ],
        axis=0,
    ).reshape(8 * capacity, narrow)
    result = lax.dot_general(picker, returned, (((0,), (0,)), ((), ())), preferred_element_type=F32)
    return result.astype(BF)


def solution(mesh):
    placed = (
        P(("exp", "row"), "col"),
        P(("exp", "row"), None),
        P(("exp", "row"), None),
        P("exp", None, ("row", "col")),
        P("exp", None, ("row", "col")),
        P("exp", ("row", "col"), None),
        P(None, None, "exp", None, ("row", "col")),
        P(None, None, "exp", None, ("row", "col")),
        P(None, None, None, "exp", None),
    )
    return jax.shard_map(
        body, mesh=mesh, in_specs=placed, out_specs=P(("exp", "row"), "col"), check_vma=False
    )
```
